32 devices in a mesh: groups: 2 (over x), blk: 16 (over z, y, core).
Axes of the slice: x: 2, y: 2, z: 4, core: 2. Of those that a mesh axis runs over, the one named last changes fastest.
Arguments:
- query_inputs: bfloat16 [8192, 4096], P(('groups', 'blk')), parts along dimension 0, may hold values from -6 to 6
- query_grads: bfloat16 [8192, 4096], P(('groups', 'blk')), parts along dimension 0, may hold values from -6 to 6
- proj_in: bfloat16 [4096, 64], replicated, may hold values from -0.09375 to 0.09375
- proj_out: bfloat16 [4096, 64], replicated, may hold values from -0.09375 to 0.09375
- train_rows: bfloat16 [8192, 4096], P(('groups', 'blk')), parts along dimension 0, may hold values from -0.09375 to 0.09375
- token_owner: int32 [8192, 1], P(('groups', 'blk')), parts along dimension 0, may hold values from 0 to 15; in each aligned block of 256 rows (0 to 255, 256 to 511, ...) at most 64 rows name the same one
- token_slot: int32 [8192], P(('groups', 'blk')), parts along dimension 0, may hold values from 0 to 31
Outputs:
- influence: bfloat16 [12, 32, 8192], P(None, None, ('groups', 'blk')), parts along dimension 2
The draws below stay inside these ranges and needn't reach their ends.
There are 2 independent parts, one for each index of `groups`. The reference program is written for one: setup_inputs(seed, part) draws one part's arguments, and reference() takes and returns one part's arrays. A program takes and returns all parts, laid end to end along the dimension named above; an argument that names none is the same for every part. Nothing has to cross between parts.
Inputs may be any that keep to these rules, and one draw needn't show every extreme that they name: `token_owner`: within the tokens of one device no owner is named by more than 64 tokens, a bound that some block reaches.
All inputs are finite; a program needn't handle non-finite values. Where the reference program divides by a largest or mean magnitude, that divisor is 1e-20 or more.
Results may differ from the reference program's by a relative error of at most 0.0069.
Values may be sent and summed in bfloat16 or wider, within the bound.
No kernel may reach another device: no remote copies, remote signals or barrier semaphores. Data moves between devices by JAX's collectives and lax.ppermute only.
A program may use at most 64 MiB of HBM per device.

```python
import math
import jax
import jax.numpy as jnp
import numpy as np
from jax import lax

D = 4096
R = 64
TOK_DEV = 256
DOC_DEV = 32
TR_DEV = 256
STOPS = 12
NEWTON_STEPS = 6
LEAD = 5
OWNERS = 16
CAP = 64
TOKENS = 4096
TRAIN = 4096


def place_ends(array, stream_key, least, high):
    spot = [jax.random.randint(jax.random.fold_in(stream_key, axis), (), 0, length) for axis, length in enumerate(array.shape)]
    main_axis = array.shape.index(max(array.shape))
    beside = spot[:main_axis] + [(spot[main_axis] + 1) % array.shape[main_axis]] + spot[main_axis + 1:]
    return array.at[tuple(spot)].set(least).at[tuple(beside)].set(high)


def level_of(key, dims, cuts, low, top_value):
    def one(position, blocks):
        draws = jax.random.uniform(jax.random.fold_in(jax.random.fold_in(key, 6), position), (blocks,), jnp.float32, low / len(cuts), top_value / len(cuts))
        return jnp.repeat(jnp.exp(draws), dims[position] // blocks).reshape((-1,) + (1,) * (len(dims) - position - 1))

    factor_of = one(*cuts[0])
    for cut in cuts[1:]:
        factor_of = factor_of * one(*cut)
    return factor_of


def deal_out(stream_key, own, number, rows, count, top, limit, skew):
    ranking = jax.random.permutation(stream_key, count)
    crowded, common = load_shares(count, rows * top, limit, skew, True), load_shares(count, rows * top, limit, skew, False)
    places = jnp.arange(count)

    def named(sizes, offset_by):
        used = int((sizes > 0).sum())
        fixed = max(1, used // 4)
        passed = fixed + (places - fixed + offset_by * (used - fixed)) % max(1, count - fixed)
        return jnp.zeros((count,), jnp.int32).at[ranking[jnp.where(places < fixed, places, passed)]].set(jnp.asarray(sizes, jnp.int32))

    sizes = jnp.where(number % 4 == 0, named(crowded, number // 4), named(common, number - number // 4 - 1))
    mixed = jax.random.permutation(jax.random.fold_in(own, 3), count)
    giver, receiver = mixed[0:count // 2 * 2:2], mixed[1:count // 2 * 2:2]
    slack = jnp.minimum(sizes[giver] - 1, limit - sizes[receiver]) // 2
    slack = jnp.where((giver == ranking[0]) | (receiver == ranking[0]) | (sizes[receiver] == 0), 0, jnp.maximum(slack, 0))
    passed = jax.random.randint(jax.random.fold_in(own, 4), (count // 2,), 0, 1 << 20) % (slack + 1)
    sizes = sizes.at[giver].add(-passed).at[receiver].add(passed)
    labels = jnp.searchsorted(jnp.cumsum(sizes), jnp.arange(rows * top), side="right").astype(jnp.int32)
    table = labels.reshape(top, rows).T
    table = table[jax.random.permutation(jax.random.fold_in(own, 1), rows)]
    offset_by = jax.random.randint(jax.random.fold_in(own, 2), (rows, 1), 0, top)
    return jnp.take_along_axis(table, (jnp.arange(top)[None, :] + offset_by) % top, axis=1)


def load_shares(amount, total, reach, lean, full):
    portions = [(1 << 20) // math.isqrt(standing ** lean) + 1 for standing in range(1, amount + 1)]
    largest = reach if full else min(reach, max(-(-total // amount), total * portions[0] // sum(portions)))
    least = 1 if total - largest >= amount - 1 else 0
    holding, spare = [largest] + [least] * (amount - 1), total - largest - least * (amount - 1)
    while spare > 0:
        candidates = [i for i in range(1, amount) if holding[i] < largest] or [i for i in range(1, amount) if holding[i] < reach]
        mass, left = sum([portions[i] for i in candidates]), spare
        for i in candidates:
            extra = min(reach - holding[i], max(1, left * portions[i] // mass), spare)
            holding[i] = holding[i] + extra
            spare = spare - extra
    return np.array(holding)


def bell_draw(key, extent, deviation, bound, cuts=(), held_as=jnp.bfloat16):
    drawn = deviation * jax.random.normal(key, extent, jnp.float32)
    if cuts:
        drawn = drawn * level_of(key, extent, cuts, -0.22, 0.18)
    return jnp.clip(drawn, -bound, bound).astype(held_as)


def setup_inputs(seed: int = 0, part: int = 0) -> dict:
    seeds = jax.random.split(jax.random.key(seed), 8)
    part_keys = jax.random.split(jax.random.fold_in(seeds[7], part), 8)
    query_inputs = bell_draw(part_keys[0], (TOKENS, D), 1.0, 6.0, ((0, 16),))
    query_grads = bell_draw(part_keys[1], (TOKENS, D), 1.0, 6.0, ((0, 16),))
    proj_in = bell_draw(seeds[2], (D, R), D ** -0.5, 0.09375)
    proj_out = bell_draw(seeds[3], (D, R), D ** -0.5, 0.09375)
    train_rows = bell_draw(part_keys[4], (TRAIN, R * R), (R * R) ** -0.5, 0.09375, ((0, 16),))
    token_owner_keys = jax.random.split(jax.random.fold_in(part_keys[5], 1), TOKENS // TOK_DEV)
    token_owner_turns = jax.random.permutation(jax.random.fold_in(part_keys[5], 3), TOKENS // TOK_DEV)
    token_owner = jax.vmap(lambda own, number: deal_out(jax.random.fold_in(part_keys[5], 2), own, number, TOK_DEV, OWNERS, 1, CAP, 2))(token_owner_keys, token_owner_turns).reshape((TOKENS, 1))
    token_slot = place_ends(jax.random.randint(part_keys[6], (TOKENS,), 0, DOC_DEV), jax.random.fold_in(part_keys[6], 1), 0, DOC_DEV - 1).astype(jnp.int32)
    return {"query_inputs": query_inputs, "query_grads": query_grads, "proj_in": proj_in, "proj_out": proj_out, "train_rows": train_rows, "token_owner": token_owner, "token_slot": token_slot}


HIGHEST_PRECISION = lax.Precision.HIGHEST


def inverse_factor(gram_sum, counts):
    width_low = gram_sum.shape[1]
    identity_mat = jnp.eye(width_low, dtype=jnp.float32)
    damped = gram_sum / (counts[:, None, None] + 1.0) + identity_mat[None]
    row_bound = jnp.max(jnp.sum(jnp.abs(damped), axis=2), axis=1)
    approx = identity_mat[None] / row_bound[:, None, None]
    for iteration in range(NEWTON_STEPS):
        product = jnp.einsum("dab,dbc->dac", damped, approx, precision=HIGHEST_PRECISION)
        approx = jnp.einsum("dab,dbc->dac", approx, 2.0 * identity_mat[None] - product, precision=HIGHEST_PRECISION)
    return approx


def reference(query_inputs, query_grads, proj_in, proj_out, train_rows, token_owner, token_slot):
    grads_low = jnp.dot(query_grads, proj_out, preferred_element_type=jnp.float32).astype(jnp.bfloat16)
    inputs_low = jnp.dot(query_inputs, proj_in, preferred_element_type=jnp.float32).astype(jnp.bfloat16)
    doc_ids = (token_owner[:, 0] * DOC_DEV + token_slot).astype(jnp.int32)
    doc_total = OWNERS * DOC_DEV

    def accumulate(carried, index):
        grad_sum, input_sum, count_sum = carried
        start = (index * TOK_DEV).astype(jnp.int32)
        grads_part = lax.dynamic_slice_in_dim(grads_low, start, TOK_DEV, 0).astype(jnp.float32)
        inputs_part = lax.dynamic_slice_in_dim(inputs_low, start, TOK_DEV, 0).astype(jnp.float32)
        ids_part = lax.dynamic_slice_in_dim(doc_ids, start, TOK_DEV, 0)
        joined = jnp.concatenate([grads_part, inputs_part], axis=1)
        grad_terms = grads_part[:, :, None] * joined[:, None, :]
        input_terms = inputs_part[:, :, None] * inputs_part[:, None, :]
        grad_sum = grad_sum.at[ids_part].add(grad_terms)
        input_sum = input_sum.at[ids_part].add(input_terms)
        count_sum = count_sum.at[ids_part].add(jnp.ones((TOK_DEV,), jnp.float32))
        return (grad_sum, input_sum, count_sum), None

    start_sums = (jnp.zeros((doc_total, R, 2 * R), jnp.float32), jnp.zeros((doc_total, R, R), jnp.float32), jnp.zeros((doc_total,), jnp.float32))
    sums_done, unused = lax.scan(accumulate, start_sums, jnp.arange(OWNERS, dtype=jnp.int32))
    grad_sum, input_sum, count_sum = sums_done
    outer_b = grad_sum[:, :, :R]
    doc_grad = grad_sum[:, :, R:]
    inv_a = inverse_factor(input_sum, count_sum)
    inv_b = inverse_factor(outer_b, count_sum)
    tilted = jnp.einsum("dab,dbc->dac", inv_b, doc_grad, precision=HIGHEST_PRECISION)
    tilted = jnp.einsum("dab,dbc->dac", tilted, inv_a, precision=HIGHEST_PRECISION)
    queries = tilted.reshape(OWNERS, DOC_DEV, R * R).astype(jnp.bfloat16)
    train_blocks = train_rows.reshape(OWNERS, TR_DEV, R * R)
    offsets = jnp.arange(STOPS, dtype=jnp.int32)

    def one_device(index):
        sources = (index - offsets + LEAD) % OWNERS
        visiting = queries[sources].astype(jnp.float32)
        resident = train_blocks[index].astype(jnp.float32)
        return jnp.einsum("skf,tf->skt", visiting, resident).astype(jnp.bfloat16)

    tile_rows = lax.map(one_device, jnp.arange(OWNERS, dtype=jnp.int32))
    return jnp.transpose(tile_rows, (1, 2, 0, 3)).reshape(STOPS, DOC_DEV, OWNERS * TR_DEV)
```

```python
import functools
import jax
import jax.numpy as jnp
import numpy as np
from jax import lax
from jax.experimental import pallas as pl
from jax.experimental.pallas import tpu as pltpu
from jax.sharding import PartitionSpec as P

DOC_DEV = 32
STOPS = 12
NEWTON_STEPS = 6
LEAD = 5
TAIL = 16
F32 = jnp.float32
BF16 = jnp.bfloat16
HIGHEST_PRECISION = lax.Precision.HIGHEST


def pack_kernel(inputs_ref, grads_ref, pin_ref, pout_ref, owner_ref, slot_ref, send_ref, ilow_ref, glow_ref):
    step = pl.program_id(0)

    @pl.when(step == 0)
    def _():
        ilow_ref[...] = jnp.zeros_like(ilow_ref)
        glow_ref[...] = jnp.zeros_like(glow_ref)

    ilow_ref[...] += jnp.dot(inputs_ref[...], pin_ref[...], preferred_element_type=F32)
    glow_ref[...] += jnp.dot(grads_ref[...], pout_ref[...], preferred_element_type=F32)

    @pl.when(step == pl.num_programs(0) - 1)
    def _():
        owners, per, wide = send_ref.shape
        cap = per - TAIL
        toks = slot_ref.shape[1]
        low = jnp.concatenate([glow_ref[...], ilow_ref[...]], axis=1).astype(BF16)
        owner_col = owner_ref[...]
        hot = (owner_col == lax.broadcasted_iota(jnp.int32, (toks, owners), 1)).astype(F32)
        tri = lax.broadcasted_iota(jnp.int32, (toks, toks), 0) > lax.broadcasted_iota(jnp.int32, (toks, toks), 1)
        before = jnp.dot(tri.astype(F32).astype(BF16), hot.astype(BF16), preferred_element_type=F32)
        rank = jnp.sum(before * hot, axis=1, keepdims=True)
        both = jnp.concatenate(
            [jnp.broadcast_to(rank, (toks, wide)), jnp.broadcast_to(owner_col.astype(F32), (toks, wide))], axis=1
        ).T
        rank_row = both[:1]
        owner_row = both[wide : wide + 1]
        position = (owner_row * cap + rank_row).astype(jnp.int32)
        placed = lax.broadcasted_iota(jnp.int32, (owners * cap, toks), 0) == position
        rows = jnp.dot(placed.astype(F32).astype(BF16), low, preferred_element_type=F32).astype(BF16)
        hot_row = owner_row == lax.broadcasted_iota(jnp.int32, (owners, toks), 0).astype(F32)
        named = jnp.where(hot_row, slot_ref[...].astype(F32) + 1.0, 0.0).astype(BF16)
        lane = lax.broadcasted_iota(jnp.int32, (toks, wide), 1) % cap
        at_lane = (rank.astype(jnp.int32) == lane).astype(F32).astype(BF16)
        slots = jnp.dot(named, at_lane, preferred_element_type=F32).astype(BF16)
        for o in range(owners):
            send_ref[o, :cap, :] = rows[o * cap : (o + 1) * cap]
            send_ref[o, cap:, :] = jnp.broadcast_to(slots.astype(F32)[o : o + 1], (TAIL, wide)).astype(BF16)


def packed_rows(query_inputs, query_grads, proj_in, proj_out, token_owner, token_slot, owners, cap):
    toks, width = query_inputs.shape
    low = proj_in.shape[1]
    steps = 4
    part = width // steps
    return pl.pallas_call(
        pack_kernel,
        grid=(steps,),
        out_shape=jax.ShapeDtypeStruct((owners, cap + TAIL, 2 * low), BF16),
        in_specs=[
            pl.BlockSpec((toks, part), lambda i: (0, i)),
            pl.BlockSpec((toks, part), lambda i: (0, i)),
            pl.BlockSpec((part, low), lambda i: (i, 0)),
            pl.BlockSpec((part, low), lambda i: (i, 0)),
            pl.BlockSpec((toks, 1), lambda i: (0, 0)),
            pl.BlockSpec((1, toks), lambda i: (0, 0)),
        ],
        out_specs=pl.BlockSpec((owners, cap + TAIL, 2 * low), lambda i: (0, 0, 0)),
        scratch_shapes=[pltpu.VMEM((toks, low), F32), pltpu.VMEM((toks, low), F32)],
        compiler_params=pltpu.CompilerParams(vmem_limit_bytes=40 * 2**20),
    )(query_inputs, query_grads, proj_in, proj_out, token_owner, token_slot.reshape(1, toks))


def split(value, parts):
    out = []
    for _ in range(parts):
        top = value.astype(BF16)
        out.append(top)
        value = value - top.astype(F32)
    return out


def times(left, right):
    rows = left.shape[0]
    parts = split(left, len(right))
    total = None
    for order, piece in enumerate(right):
        used = parts[: len(right) - order]
        got = jnp.dot(jnp.concatenate(used, axis=0), piece, preferred_element_type=F32)
        for j in range(len(used)):
            term = got[j * rows : (j + 1) * rows]
            total = term if total is None else total + term
    return total


def on_diagonal(wide, parts):
    rows = wide.shape[0]
    pair = wide.shape[1] // 2
    first = lax.broadcasted_iota(jnp.int32, (rows, pair), 1) < rows
    zero = jnp.zeros((rows, pair), BF16)
    out = []
    for part in split(wide, parts):
        ahead, after = part[:, :pair], part[:, pair:]
        none = jnp.zeros_like(ahead)
        out.append(
            jnp.concatenate(
                [
                    jnp.concatenate([jnp.where(first, ahead, none), zero], axis=1),
                    jnp.concatenate([jnp.where(first, none, ahead), zero], axis=1),
                    jnp.concatenate([zero, jnp.where(first, after, none)], axis=1),
                    jnp.concatenate([zero, jnp.where(first, none, after)], axis=1),
                ],
                axis=0,
            )
        )
    return out


def query_kernel(first_doc, recv_ref, out_ref, gram_ref, rows_ref, count_ref):
    docs, low, _ = out_ref.shape
    sources, per, wide = recv_ref.shape
    cap = per - TAIL
    rows = jnp.concatenate([recv_ref[s, :cap, :] for s in range(sources)], axis=0)
    rows_ref[...] = rows.T
    half = lax.broadcasted_iota(jnp.int32, (1, wide), 1) < low
    named = [recv_ref[s, cap:, :].astype(F32)[:1] for s in range(sources)]
    slot = jnp.concatenate([jnp.where(half, named[s], named[s + 1]) for s in range(0, sources, 2)], axis=1)
    across = rows_ref[...]
    for d in range(docs):
        mine = (slot == (first_doc + d + 1)).astype(F32)
        gram_ref[d] = jnp.dot(across * mine.astype(BF16), rows, preferred_element_type=F32)
        count_ref[d : d + 1, :] = jnp.broadcast_to(jnp.sum(mine, axis=1, keepdims=True), (1, wide))

    row_at = lax.broadcasted_iota(jnp.int32, (low, wide), 0)
    lane_at = lax.broadcasted_iota(jnp.int32, (low, wide), 1)
    first = lane_at < low
    eye = ((row_at == lane_at) | (row_at + low == lane_at)).astype(F32)
    eyes = jnp.concatenate([eye, eye], axis=1)
    powers, scales, mixed = [], [], []
    for g in range(0, docs, 2):
        errors, inverses, grads = [], [], []
        for d in (g, g + 1):
            both = gram_ref[d]
            outer = jnp.where(first, both[:low], both[low:])
            damped = outer / (count_ref[d : d + 1, :] + 1.0) + eye
            sums = jnp.sum(jnp.abs(damped), axis=0, keepdims=True)
            bound_b = jnp.max(jnp.where(half, sums, 0.0), axis=1, keepdims=True)
            bound_a = jnp.max(jnp.where(half, 0.0, sums), axis=1, keepdims=True)
            inverse = 1.0 / jnp.where(half, bound_b, bound_a)
            errors.append(eye - damped * inverse)
            inverses.append(inverse)
            grads.append(jnp.where(first, 0.0, both[:low]))
        powers.append(jnp.concatenate(errors, axis=1))
        scales.append(jnp.concatenate(inverses, axis=1))
        mixed.append(grads)
    totals = [eyes + power for power in powers]
    powers = [times(power, on_diagonal(power, 2)) for power in powers]
    for _ in range(NEWTON_STEPS - 2):
        stepped = [
            times(jnp.concatenate([power, total], axis=0), on_diagonal(power, 2))
            for power, total in zip(powers, totals)
        ]
        powers = [both[:low] for both in stepped]
        totals = [total + both[low:] for total, both in zip(totals, stepped)]
    totals = [total + times(total, on_diagonal(power, 2)) for power, total in zip(powers, totals)]
    totals = [total * scale for total, scale in zip(totals, scales)]
    tilted = []
    for total, grads in zip(totals, mixed):
        right = []
        gap = jnp.zeros((low, 2 * wide), BF16)
        zero = jnp.zeros((low, wide), BF16)
        for ahead, after in zip(split(grads[0], 3), split(grads[1], 3)):
            right.append(
                jnp.concatenate(
                    [jnp.concatenate([ahead, zero], axis=1), gap, jnp.concatenate([zero, after], axis=1), gap], axis=0
                )
            )
        tilted.append(times(total, right))
    found = [times(tilt, on_diagonal(total, 3)) for tilt, total in zip(tilted, totals)]
    for g, query in enumerate(found):
        out_ref[2 * g] = query[:, low:wide].astype(BF16)
        out_ref[2 * g + 1] = query[:, wide + low :].astype(BF16)


def queries_of(recv, first_doc, docs, low):
    sources, per, wide = recv.shape
    found = pl.pallas_call(
        functools.partial(query_kernel, first_doc),
        out_shape=jax.ShapeDtypeStruct((docs, low, low), BF16),
        in_specs=[pl.BlockSpec(memory_space=pltpu.VMEM)],
        out_specs=pl.BlockSpec(memory_space=pltpu.VMEM),
        scratch_shapes=[
            pltpu.VMEM((docs, wide, wide), F32),
            pltpu.VMEM((wide, sources * (per - TAIL)), BF16),
            pltpu.VMEM((docs, wide), F32),
        ],
        cost_estimate=pl.CostEstimate(flops=4 * 10**9, bytes_accessed=2**20, transcendentals=0),
        compiler_params=pltpu.CompilerParams(vmem_limit_bytes=40 * 2**20),
    )(recv)
    return found.reshape(docs, low * low)


def order_kernel(from_ref, *refs):
    chunks = (len(refs) - 1) // 2
    out_ref = refs[-1]
    docs = refs[0].shape[1]
    blocks = refs[0].shape[0]
    for k in range(out_ref.shape[0]):
        place = from_ref[k]

        @pl.when(place < blocks)
        def _():
            for c in range(chunks):
                out_ref[k, c * docs : (c + 1) * docs, :] = refs[2 * c][place]

        @pl.when(place >= blocks)
        def _():
            for c in range(chunks):
                out_ref[k, c * docs : (c + 1) * docs, :] = refs[2 * c + 1][place - blocks]


def ring_tables(owners):
    chips = owners // 2
    line = chips // 2
    chip_at = [2 * p if p < line else 2 * (chips - 1 - p) + 1 for p in range(chips)]
    spot = {m: p for p, m in enumerate(chip_at)}
    pairs = []
    for p in range(chips):
        pairs.append((2 * chip_at[p], 2 * chip_at[(p + 1) % chips]))
        pairs.append((2 * chip_at[p] + 1, 2 * chip_at[(p - 1) % chips] + 1))
    held = {}
    for device in range(owners):
        m, core = divmod(device, 2)
        sign = -1 if core == 0 else 1
        listed = [device]
        for hop in range(1, chips // 2):
            there = chip_at[(spot[m] + sign * hop) % chips]
            listed += [2 * there, 2 * there + 1]
        listed.append(2 * chip_at[(spot[m] + sign * (chips // 2)) % chips] + core)
        held[device] = listed
    where = np.zeros((owners, STOPS), np.int32)
    for device in range(owners):
        for k in range(STOPS):
            owner = (device + LEAD - k) % owners
            if owner in held[device]:
                where[device, k] = held[device].index(owner)
            else:
                where[device, k] = chips + held[device ^ 1].index(owner)
    swap = [(device, device ^ 1) for device in range(owners)]
    return pairs, swap, where


def gathered(query_inputs, query_grads, proj_in, proj_out, train_rows, token_owner, token_slot):
    toks = query_inputs.shape[0]
    low = proj_in.shape[1]
    owners = lax.axis_size("blk")
    chips = owners // 2
    train = train_rows.shape[0]
    cap = 4 * toks // owners
    ring, swap, where = ring_tables(owners)
    place = lax.axis_index("blk")
    odd = lax.rem(place, 2) == 1
    from_where = jnp.asarray(where)[place]

    other_rows = lax.ppermute(train_rows, "blk", swap)
    both_rows = jnp.concatenate([train_rows, other_rows], axis=0)

    send = packed_rows(query_inputs, query_grads, proj_in, proj_out, token_owner, token_slot, owners, cap)
    recv = lax.all_to_all(send, "blk", split_axis=0, concat_axis=0, tiled=True)

    def scoring(block):
        return lax.dot_general(
            block, both_rows, (((1,), (1,)), ((), ())), preferred_element_type=F32
        ).astype(BF16)

    chunks = 2
    docs = DOC_DEV // chunks
    results = []
    for c in range(chunks):
        mine = queries_of(recv, c * docs, docs, low)
        theirs = lax.ppermute(mine, "blk", swap)
        even_block = jnp.where(odd, theirs, mine)
        odd_block = jnp.where(odd, mine, theirs)
        travelling = jnp.concatenate([even_block, odd_block], axis=0)
        tiles = [scoring(mine)]
        for hop in range(1, chips // 2):
            travelling = lax.ppermute(travelling, "blk", ring)
            tiles.append(scoring(travelling))
        last = jnp.where(odd, travelling[docs:], travelling[:docs])
        tiles.append(scoring(lax.ppermute(last, "blk", ring)))
        tiles = jnp.concatenate(tiles, axis=0).reshape(chips, docs, 2 * train)
        own_tiles = tiles[:, :, :train]
        results += [own_tiles, lax.ppermute(tiles[:, :, train:], "blk", swap)]
    return pl.pallas_call(
        order_kernel,
        out_shape=jax.ShapeDtypeStruct((STOPS, DOC_DEV, train), BF16),
        in_specs=[pl.BlockSpec(memory_space=pltpu.SMEM)] + [pl.BlockSpec(memory_space=pltpu.VMEM)] * (2 * chunks),
        out_specs=pl.BlockSpec(memory_space=pltpu.VMEM),
    )(from_where, *results)
def passed_along(value, axis, steps):
    count = lax.axis_size(axis)
    pairs = [(source, (source + steps) % count) for source in range(count)]
    return lax.ppermute(value, axis, pairs)


def inverse_factor(gram_sum, counts):
    width_low = gram_sum.shape[1]
    identity_mat = jnp.eye(width_low, dtype=jnp.float32)
    damped = gram_sum / (counts[:, None, None] + 1.0) + identity_mat[None]
    row_bound = jnp.max(jnp.sum(jnp.abs(damped), axis=2), axis=1)
    approx = identity_mat[None] / row_bound[:, None, None]
    for iteration in range(NEWTON_STEPS):
        product = jnp.einsum("dab,dbc->dac", damped, approx, precision=HIGHEST_PRECISION)
        approx = jnp.einsum(
            "dab,dbc->dac", approx, 2.0 * identity_mat[None] - product, precision=HIGHEST_PRECISION
        )
    return approx


def passed(query_inputs, query_grads, proj_in, proj_out, train_rows, token_owner, token_slot):
    tok_count = query_inputs.shape[0]
    width_low = proj_in.shape[1]
    owners = lax.axis_size("blk")
    capacity = 4 * tok_count // owners
    grads_low = jnp.dot(query_grads, proj_out, preferred_element_type=jnp.float32).astype(
        jnp.bfloat16
    )
    inputs_low = jnp.dot(query_inputs, proj_in, preferred_element_type=jnp.float32).astype(
        jnp.bfloat16
    )
    low_rows = jnp.concatenate([grads_low, inputs_low], axis=1)
    owner_ids = token_owner[:, 0]
    owner_hot = (owner_ids[:, None] == jnp.arange(owners, dtype=jnp.int32)[None, :]).astype(
        jnp.float32
    )
    tok_index = jnp.arange(tok_count, dtype=jnp.int32)
    earlier = (tok_index[:, None] > tok_index[None, :]).astype(jnp.float32)
    before = jnp.dot(earlier, owner_hot, precision=HIGHEST_PRECISION)
    rank_in = jnp.sum(before * owner_hot, axis=1).astype(jnp.int32)
    position = owner_ids * capacity + rank_in
    slot_index = jnp.arange(owners * capacity, dtype=jnp.int32)
    placed = slot_index[:, None] == position[None, :]
    send_rows = jnp.dot(
        placed.astype(jnp.bfloat16), low_rows, preferred_element_type=jnp.float32
    ).astype(jnp.bfloat16)
    send_slot = jnp.sum(jnp.where(placed, token_slot[None, :] + 1, 0), axis=1)
    recv_rows, recv_slot = (
        lax.all_to_all(
            send_rows.reshape(owners, capacity, 2 * width_low),
            "blk",
            split_axis=0,
            concat_axis=0,
            tiled=True,
        ),
        lax.all_to_all(
            send_slot.reshape(owners, capacity), "blk", split_axis=0, concat_axis=0, tiled=True
        ),
    )
    recv_rows = recv_rows.reshape(owners * capacity, 2 * width_low)
    recv_slot = recv_slot.reshape(owners * capacity)
    doc_index = jnp.arange(1, DOC_DEV + 1, dtype=jnp.int32)
    doc_hot = recv_slot[:, None] == doc_index[None, :]
    counts = jnp.sum(doc_hot.astype(jnp.float32), axis=0)
    hot_bf = doc_hot.astype(jnp.bfloat16)
    grads_recv = recv_rows[:, :width_low]
    inputs_recv = recv_rows[:, width_low:]
    spread_grads = (hot_bf[:, :, None] * grads_recv[:, None, :]).reshape(
        owners * capacity, DOC_DEV * width_low
    )
    spread_inputs = (hot_bf[:, :, None] * inputs_recv[:, None, :]).reshape(
        owners * capacity, DOC_DEV * width_low
    )
    contract = (((0,), (0,)), ((), ()))
    grad_gram = lax.dot_general(
        spread_grads, recv_rows, contract, preferred_element_type=jnp.float32
    ).reshape(DOC_DEV, width_low, 2 * width_low)
    outer_b = grad_gram[:, :, :width_low]
    doc_grad = grad_gram[:, :, width_low:]
    outer_a = lax.dot_general(
        spread_inputs, inputs_recv, contract, preferred_element_type=jnp.float32
    ).reshape(DOC_DEV, width_low, width_low)
    inv_a = inverse_factor(outer_a, counts)
    inv_b = inverse_factor(outer_b, counts)
    tilted = jnp.einsum("dab,dbc->dac", inv_b, doc_grad, precision=HIGHEST_PRECISION)
    tilted = jnp.einsum("dab,dbc->dac", tilted, inv_a, precision=HIGHEST_PRECISION)
    queries = tilted.reshape(DOC_DEV, width_low * width_low).astype(jnp.bfloat16)
    score_dims = (((1,), (1,)), ((), ()))

    def scoring(block):
        return lax.dot_general(
            block, train_rows, score_dims, preferred_element_type=jnp.float32
        ).astype(jnp.bfloat16)

    def step_ahead(current_block, unused):
        arrived = passed_along(current_block, "blk", 1)
        return (arrived, scoring(arrived))

    def step_back(current_block):
        arrived = passed_along(current_block, "blk", -1)
        return (arrived, scoring(arrived))

    def both_ways(carried, unused):
        ahead_block, back_block = carried
        ahead_block, ahead_tile = step_ahead(ahead_block, unused)
        back_block, back_tile = step_back(back_block)
        return ((ahead_block, back_block), (ahead_tile, back_tile))

    last_pair, paired_tiles = lax.scan(both_ways, (queries, queries), None, length=LEAD)
    ahead_tiles, back_tiles = paired_tiles
    tail_block, tail_tiles = lax.scan(step_ahead, last_pair[0], None, length=STOPS - 1 - 2 * LEAD)
    stacked = jnp.concatenate(
        [jnp.flip(back_tiles, 0), scoring(queries)[None], ahead_tiles, tail_tiles], axis=0
    )
    return stacked


def solution(mesh):
    owners = mesh.shape["blk"]

    def local(query_inputs, query_grads, proj_in, *rest):
        low = proj_in.shape[1]
        cap = 4 * query_inputs.shape[0] // owners
        close = owners % 4 == 0 and STOPS <= owners <= 2 * STOPS and cap == low and cap % TAIL == 0
        return (gathered if close else passed)(query_inputs, query_grads, proj_in, *rest)

    placed = (
        P(("groups", "blk"), None),
        P(("groups", "blk"), None),
        P(),
        P(),
        P(("groups", "blk"), None),
        P(("groups", "blk"), None),
        P(("groups", "blk")),
    )
    return jax.shard_map(
        local,
        mesh=mesh,
        in_specs=placed,
        out_specs=P(None, None, ("groups", "blk")),
        check_vma=False,
    )
```

```python
import functools
import jax
import jax.numpy as jnp
from jax import lax
from jax.experimental import pallas as pl
from jax.experimental.pallas import tpu as pltpu
from jax.sharding import PartitionSpec as P

DOC_DEV = 32
STOPS = 12
NEWTON_STEPS = 6
LEAD = 5
TAIL = 16
F32 = jnp.float32
BF16 = jnp.bfloat16
HIGHEST_PRECISION = lax.Precision.HIGHEST
LAST_DIMS = (((1,), (1,)), ((), ()))


def pack_kernel(inputs_ref, grads_ref, pin_ref, pout_ref, owner_ref, slot_ref, send_ref, ilow_ref, glow_ref):
    step = pl.program_id(0)

    @pl.when(step == 0)
    def _():
        ilow_ref[...] = jnp.zeros_like(ilow_ref)
        glow_ref[...] = jnp.zeros_like(glow_ref)

    ilow_ref[...] += lax.dot_general(inputs_ref[...], pin_ref[...], LAST_DIMS, preferred_element_type=F32)
    glow_ref[...] += lax.dot_general(grads_ref[...], pout_ref[...], LAST_DIMS, preferred_element_type=F32)

    @pl.when(step == pl.num_programs(0) - 1)
    def _():
        owners, per, wide = send_ref.shape
        cap = per - TAIL
        toks = slot_ref.shape[1]
        low = jnp.concatenate([glow_ref[...], ilow_ref[...]], axis=1).astype(BF16)
        owner = owner_ref[...]
        hot = (owner == lax.broadcasted_iota(jnp.int32, (owners, toks), 0)).astype(F32)
        earlier = lax.broadcasted_iota(jnp.int32, (toks, toks), 0) < lax.broadcasted_iota(jnp.int32, (toks, toks), 1)
        before = jnp.dot(hot.astype(BF16), earlier.astype(F32).astype(BF16), preferred_element_type=F32)
        rank = jnp.sum(before * hot, axis=0, keepdims=True).astype(jnp.int32)
        position = owner * cap + rank
        placed = lax.broadcasted_iota(jnp.int32, (owners * cap, toks), 0) == position
        rows = jnp.dot(placed.astype(F32).astype(BF16), low, preferred_element_type=F32).astype(BF16)
        named = (hot * (slot_ref[...].astype(F32) + 1.0)).astype(BF16)
        at_lane = lax.broadcasted_iota(jnp.int32, (wide, toks), 0) % cap == rank
        slots = lax.dot_general(named, at_lane.astype(F32).astype(BF16), LAST_DIMS, preferred_element_type=F32)
        for o in range(owners):
            send_ref[o, :cap, :] = rows[o * cap : (o + 1) * cap]
            send_ref[o, cap:, :] = jnp.broadcast_to(slots[o : o + 1], (TAIL, wide)).astype(BF16)


def packed_rows(query_inputs, query_grads, proj_in, proj_out, token_owner, token_slot, owners, cap):
    toks, width = query_inputs.shape
    low = proj_in.shape[1]
    steps = 4
    part = width // steps
    return pl.pallas_call(
        pack_kernel,
        grid=(steps,),
        out_shape=jax.ShapeDtypeStruct((owners, cap + TAIL, 2 * low), BF16),
        in_specs=[
            pl.BlockSpec((toks, part), lambda i: (0, i)),
            pl.BlockSpec((toks, part), lambda i: (0, i)),
            pl.BlockSpec((low, part), lambda i: (0, i)),
            pl.BlockSpec((low, part), lambda i: (0, i)),
            pl.BlockSpec((1, toks), lambda i: (0, 0)),
            pl.BlockSpec((1, toks), lambda i: (0, 0)),
        ],
        out_specs=pl.BlockSpec((owners, cap + TAIL, 2 * low), lambda i: (0, 0, 0)),
        scratch_shapes=[pltpu.VMEM((toks, low), F32), pltpu.VMEM((toks, low), F32)],
        compiler_params=pltpu.CompilerParams(vmem_limit_bytes=40 * 2**20),
    )(query_inputs, query_grads, proj_in.T, proj_out.T, token_owner.reshape(1, toks), token_slot.reshape(1, toks))


def split(value, parts):
    out = []
    for _ in range(parts):
        top = value.astype(BF16)
        out.append(top)
        value = value - top.astype(F32)
    return out


def times(left, right):
    rows = left.shape[0]
    parts = split(left, len(right))
    total = None
    for order, piece in enumerate(right):
        used = parts[: len(right) - order]
        got = jnp.dot(jnp.concatenate(used, axis=0), piece, preferred_element_type=F32)
        for j in range(len(used)):
            term = got[j * rows : (j + 1) * rows]
            total = term if total is None else total + term
    return total


def on_diagonal(wide, parts):
    rows = wide.shape[0]
    pair = wide.shape[1] // 2
    first = lax.broadcasted_iota(jnp.int32, (rows, pair), 1) < rows
    zero = jnp.zeros((rows, pair), BF16)
    out = []
    for part in split(wide, parts):
        ahead, after = part[:, :pair], part[:, pair:]
        none = jnp.zeros_like(ahead)
        out.append(
            jnp.concatenate(
                [
                    jnp.concatenate([jnp.where(first, ahead, none), zero], axis=1),
                    jnp.concatenate([jnp.where(first, none, ahead), zero], axis=1),
                    jnp.concatenate([zero, jnp.where(first, after, none)], axis=1),
                    jnp.concatenate([zero, jnp.where(first, none, after)], axis=1),
                ],
                axis=0,
            )
        )
    return out


def query_kernel(first_doc, recv_ref, out_ref, gram_ref, rows_ref, count_ref):
    docs, low, _ = out_ref.shape
    sources, per, wide = recv_ref.shape
    cap = per - TAIL
    rows = jnp.concatenate([recv_ref[s, :cap, :] for s in range(sources)], axis=0)
    rows_ref[...] = rows.T
    half = lax.broadcasted_iota(jnp.int32, (1, wide), 1) < low
    named = [recv_ref[s, cap:, :].astype(F32)[:1] for s in range(sources)]
    slot = jnp.concatenate([jnp.where(half, named[s], named[s + 1]) for s in range(0, sources, 2)], axis=1)
    across = rows_ref[...]
    for d in range(docs):
        mine = (slot == (first_doc + d + 1)).astype(F32)
        gram_ref[d] = jnp.dot(across * mine.astype(BF16), rows, preferred_element_type=F32)
        count_ref[d : d + 1, :] = jnp.broadcast_to(jnp.sum(mine, axis=1, keepdims=True), (1, wide))

    row_at = lax.broadcasted_iota(jnp.int32, (low, wide), 0)
    lane_at = lax.broadcasted_iota(jnp.int32, (low, wide), 1)
    first = lane_at < low
    eye = ((row_at == lane_at) | (row_at + low == lane_at)).astype(F32)
    eyes = jnp.concatenate([eye, eye], axis=1)
    powers, scales, mixed = [], [], []
    for g in range(0, docs, 2):
        errors, inverses, grads = [], [], []
        for d in (g, g + 1):
            both = gram_ref[d]
            outer = jnp.where(first, both[:low], both[low:])
            damped = outer / (count_ref[d : d + 1, :] + 1.0) + eye
            sums = jnp.sum(jnp.abs(damped), axis=0, keepdims=True)
            bound_b = jnp.max(jnp.where(half, sums, 0.0), axis=1, keepdims=True)
            bound_a = jnp.max(jnp.where(half, 0.0, sums), axis=1, keepdims=True)
            inverse = 1.0 / jnp.where(half, bound_b, bound_a)
            errors.append(eye - damped * inverse)
            inverses.append(inverse)
            grads.append(jnp.where(first, 0.0, both[:low]))
        powers.append(jnp.concatenate(errors, axis=1))
        scales.append(jnp.concatenate(inverses, axis=1))
        mixed.append(grads)
    totals = [eyes + power for power in powers]
    powers = [times(power, on_diagonal(power, 2)) for power in powers]
    for _ in range(NEWTON_STEPS - 2):
        stepped = [
            times(jnp.concatenate([power, total], axis=0), on_diagonal(power, 2))
            for power, total in zip(powers, totals)
        ]
        powers = [both[:low] for both in stepped]
        totals = [total + both[low:] for total, both in zip(totals, stepped)]
    totals = [total + times(total, on_diagonal(power, 2)) for power, total in zip(powers, totals)]
    totals = [total * scale for total, scale in zip(totals, scales)]
    tilted = []
    for total, grads in zip(totals, mixed):
        right = []
        gap = jnp.zeros((low, 2 * wide), BF16)
        zero = jnp.zeros((low, wide), BF16)
        for ahead, after in zip(split(grads[0], 3), split(grads[1], 3)):
            right.append(
                jnp.concatenate(
                    [jnp.concatenate([ahead, zero], axis=1), gap, jnp.concatenate([zero, after], axis=1), gap], axis=0
                )
            )
        tilted.append(times(total, right))
    found = [times(tilt, on_diagonal(total, 3)) for tilt, total in zip(tilted, totals)]
    for g, query in enumerate(found):
        out_ref[2 * g] = query[:, low:wide].astype(BF16)
        out_ref[2 * g + 1] = query[:, wide + low :].astype(BF16)


def queries_of(recv, first_doc, docs, low):
    sources, per, wide = recv.shape
    found = pl.pallas_call(
        functools.partial(query_kernel, first_doc),
        out_shape=jax.ShapeDtypeStruct((docs, low, low), BF16),
        in_specs=[pl.BlockSpec(memory_space=pltpu.VMEM)],
        out_specs=pl.BlockSpec(memory_space=pltpu.VMEM),
        scratch_shapes=[
            pltpu.VMEM((docs, wide, wide), F32),
            pltpu.VMEM((wide, sources * (per - TAIL)), BF16),
            pltpu.VMEM((docs, wide), F32),
        ],
        cost_estimate=pl.CostEstimate(flops=4 * 10**9, bytes_accessed=2**20, transcendentals=0),
        compiler_params=pltpu.CompilerParams(vmem_limit_bytes=40 * 2**20),
    )(recv)
    return found.reshape(docs, low * low)


def order_kernel(owners, *refs):
    chunks = (len(refs) - 1) // 2
    out_ref = refs[-1]
    docs = refs[0].shape[1]
    chips = owners // 2
    device = lax.axis_index("blk")

    def spot(chip):
        line, row = lax.div(chip, 2), lax.rem(chip, 2)
        return jnp.where(row == 0, line, chips - 1 - line)

    here, core = spot(lax.div(device, 2)), lax.rem(device, 2)
    for k in range(out_ref.shape[0]):
        owner = lax.rem(device + LEAD - k + owners, owners)
        second = lax.rem(owner, 2)
        hops = lax.rem(here - spot(lax.div(owner, 2)) + chips, chips)
        by_core = jnp.where((hops == 0) | (hops == chips // 2), second, jnp.where(hops < chips // 2, 0, 1))
        away = jnp.where(hops > chips // 2, chips - hops, hops)
        index = jnp.where(away == 0, 0, jnp.where(away == chips // 2, chips - 1, 2 * away - 1 + second))
        own = by_core == core
        for c in range(chunks):
            out_ref[k, c * docs : (c + 1) * docs, :] = jnp.where(own, refs[2 * c][index], refs[2 * c + 1][index])


def ring_pairs(owners):
    chips = owners // 2
    line = chips // 2
    chip_at = [2 * p if p < line else 2 * (chips - 1 - p) + 1 for p in range(chips)]
    pairs = []
    for p in range(chips):
        pairs.append((2 * chip_at[p], 2 * chip_at[(p + 1) % chips]))
        pairs.append((2 * chip_at[p] + 1, 2 * chip_at[(p - 1) % chips] + 1))
    return pairs, [(device, device ^ 1) for device in range(owners)]


def gathered(query_inputs, query_grads, proj_in, proj_out, train_rows, token_owner, token_slot):
    toks = query_inputs.shape[0]
    low = proj_in.shape[1]
    owners = lax.axis_size("blk")
    chips = owners // 2
    train = train_rows.shape[0]
    cap = 4 * toks // owners
    ring, swap = ring_pairs(owners)
    odd = lax.rem(lax.axis_index("blk"), 2) == 1

    send = packed_rows(query_inputs, query_grads, proj_in, proj_out, token_owner, token_slot, owners, cap)
    other_rows = lax.ppermute(train_rows, "blk", swap)
    recv = lax.all_to_all(send, "blk", split_axis=0, concat_axis=0, tiled=True)
    recv, other_rows = lax.optimization_barrier((recv, other_rows))

    def scoring(block):
        return tuple(
            lax.dot_general(block, rows, LAST_DIMS, preferred_element_type=F32).astype(BF16)
            for rows in (train_rows, other_rows)
        )

    def pair_up(mine):
        theirs = lax.ppermute(mine, "blk", swap)
        return jnp.concatenate([jnp.where(odd, theirs, mine), jnp.where(odd, mine, theirs)], axis=0)

    chunks = 2
    docs = DOC_DEV // chunks
    def onward(block, hop):
        if hop == chips // 2:
            block = jnp.where(odd, block[docs:], block[:docs])
        return lax.ppermute(block, "blk", ring)

    moving, tiles, came = [], [], []
    for c in range(chunks):
        mine = queries_of(recv, c * docs, docs, low)
        if c > 0:
            moving[c - 1] = onward(moving[c - 1], 1)
            mine, moving[c - 1] = lax.optimization_barrier((mine, moving[c - 1]))
            came.append(scoring(moving[c - 1]))
        tiles.append([scoring(mine)])
        moving.append(pair_up(mine))
        if c + 1 < chunks:
            recv, moving[c], tiles[c][0] = lax.optimization_barrier((recv, moving[c], tiles[c][0]))
    for hop in range(1, chips // 2 + 1):
        for c in range(chunks):
            if hop == 1 and c + 1 < chunks:
                continue
            block = moving[c]
            behind = len(came) - chunks - 1
            if behind >= 0:
                block, came[behind] = lax.optimization_barrier((block, came[behind]))
            moving[c] = onward(block, hop)
            came.append(scoring(moving[c]))
    for number, tile in enumerate(came):
        tiles[number % chunks].append(tile)
    results = []
    for c in range(chunks):
        own, other = (jnp.concatenate(part, axis=0).reshape(chips, docs, train) for part in zip(*tiles[c]))
        results += [own, lax.ppermute(other, "blk", swap)]
    return pl.pallas_call(
        functools.partial(order_kernel, owners),
        out_shape=jax.ShapeDtypeStruct((STOPS, DOC_DEV, train), BF16),
        in_specs=[pl.BlockSpec(memory_space=pltpu.VMEM)] * (2 * chunks),
        out_specs=pl.BlockSpec(memory_space=pltpu.VMEM),
    )(*results)


def passed_along(value, axis, steps):
    count = lax.axis_size(axis)
    pairs = [(source, (source + steps) % count) for source in range(count)]
    return lax.ppermute(value, axis, pairs)


def inverse_factor(gram_sum, counts):
    width_low = gram_sum.shape[1]
    identity_mat = jnp.eye(width_low, dtype=jnp.float32)
    damped = gram_sum / (counts[:, None, None] + 1.0) + identity_mat[None]
    row_bound = jnp.max(jnp.sum(jnp.abs(damped), axis=2), axis=1)
    approx = identity_mat[None] / row_bound[:, None, None]
    for iteration in range(NEWTON_STEPS):
        product = jnp.einsum("dab,dbc->dac", damped, approx, precision=HIGHEST_PRECISION)
        approx = jnp.einsum(
            "dab,dbc->dac", approx, 2.0 * identity_mat[None] - product, precision=HIGHEST_PRECISION
        )
    return approx


def passed(query_inputs, query_grads, proj_in, proj_out, train_rows, token_owner, token_slot):
    tok_count = query_inputs.shape[0]
    width_low = proj_in.shape[1]
    owners = lax.axis_size("blk")
    capacity = 4 * tok_count // owners
    grads_low = jnp.dot(query_grads, proj_out, preferred_element_type=jnp.float32).astype(
        jnp.bfloat16
    )
    inputs_low = jnp.dot(query_inputs, proj_in, preferred_element_type=jnp.float32).astype(
        jnp.bfloat16
    )
    low_rows = jnp.concatenate([grads_low, inputs_low], axis=1)
    owner_ids = token_owner[:, 0]
    owner_hot = (owner_ids[:, None] == jnp.arange(owners, dtype=jnp.int32)[None, :]).astype(
        jnp.float32
    )
    tok_index = jnp.arange(tok_count, dtype=jnp.int32)
    earlier = (tok_index[:, None] > tok_index[None, :]).astype(jnp.float32)
    before = jnp.dot(earlier, owner_hot, precision=HIGHEST_PRECISION)
    rank_in = jnp.sum(before * owner_hot, axis=1).astype(jnp.int32)
    position = owner_ids * capacity + rank_in
    slot_index = jnp.arange(owners * capacity, dtype=jnp.int32)
    placed = slot_index[:, None] == position[None, :]
    send_rows = jnp.dot(
        placed.astype(jnp.bfloat16), low_rows, preferred_element_type=jnp.float32
    ).astype(jnp.bfloat16)
    send_slot = jnp.sum(jnp.where(placed, token_slot[None, :] + 1, 0), axis=1)
    recv_rows, recv_slot = (
        lax.all_to_all(
            send_rows.reshape(owners, capacity, 2 * width_low),
            "blk",
            split_axis=0,
            concat_axis=0,
            tiled=True,
        ),
        lax.all_to_all(
            send_slot.reshape(owners, capacity), "blk", split_axis=0, concat_axis=0, tiled=True
        ),
    )
    recv_rows = recv_rows.reshape(owners * capacity, 2 * width_low)
    recv_slot = recv_slot.reshape(owners * capacity)
    doc_index = jnp.arange(1, DOC_DEV + 1, dtype=jnp.int32)
    doc_hot = recv_slot[:, None] == doc_index[None, :]
    counts = jnp.sum(doc_hot.astype(jnp.float32), axis=0)
    hot_bf = doc_hot.astype(jnp.bfloat16)
    grads_recv = recv_rows[:, :width_low]
    inputs_recv = recv_rows[:, width_low:]
    spread_grads = (hot_bf[:, :, None] * grads_recv[:, None, :]).reshape(
        owners * capacity, DOC_DEV * width_low
    )
    spread_inputs = (hot_bf[:, :, None] * inputs_recv[:, None, :]).reshape(
        owners * capacity, DOC_DEV * width_low
    )
    contract = (((0,), (0,)), ((), ()))
    grad_gram = lax.dot_general(
        spread_grads, recv_rows, contract, preferred_element_type=jnp.float32
    ).reshape(DOC_DEV, width_low, 2 * width_low)
    outer_b = grad_gram[:, :, :width_low]
    doc_grad = grad_gram[:, :, width_low:]
    outer_a = lax.dot_general(
        spread_inputs, inputs_recv, contract, preferred_element_type=jnp.float32
    ).reshape(DOC_DEV, width_low, width_low)
    inv_a = inverse_factor(outer_a, counts)
    inv_b = inverse_factor(outer_b, counts)
    tilted = jnp.einsum("dab,dbc->dac", inv_b, doc_grad, precision=HIGHEST_PRECISION)
    tilted = jnp.einsum("dab,dbc->dac", tilted, inv_a, precision=HIGHEST_PRECISION)
    queries = tilted.reshape(DOC_DEV, width_low * width_low).astype(jnp.bfloat16)
    score_dims = (((1,), (1,)), ((), ()))

    def scoring(block):
        return lax.dot_general(
            block, train_rows, score_dims, preferred_element_type=jnp.float32
        ).astype(jnp.bfloat16)

    def step_ahead(current_block, unused):
        arrived = passed_along(current_block, "blk", 1)
        return (arrived, scoring(arrived))

    def step_back(current_block):
        arrived = passed_along(current_block, "blk", -1)
        return (arrived, scoring(arrived))

    def both_ways(carried, unused):
        ahead_block, back_block = carried
        ahead_block, ahead_tile = step_ahead(ahead_block, unused)
        back_block, back_tile = step_back(back_block)
        return ((ahead_block, back_block), (ahead_tile, back_tile))

    last_pair, paired_tiles = lax.scan(both_ways, (queries, queries), None, length=LEAD)
    ahead_tiles, back_tiles = paired_tiles
    tail_block, tail_tiles = lax.scan(step_ahead, last_pair[0], None, length=STOPS - 1 - 2 * LEAD)
    stacked = jnp.concatenate(
        [jnp.flip(back_tiles, 0), scoring(queries)[None], ahead_tiles, tail_tiles], axis=0
    )
    return stacked


def solution(mesh):
    owners = mesh.shape["blk"]

    def local(query_inputs, query_grads, proj_in, *rest):
        low = proj_in.shape[1]
        cap = 4 * query_inputs.shape[0] // owners
        close = owners % 4 == 0 and STOPS <= owners <= 2 * STOPS and cap == low and cap % TAIL == 0
        return (gathered if close else passed)(query_inputs, query_grads, proj_in, *rest)

    placed = (
        P(("groups", "blk"), None),
        P(("groups", "blk"), None),
        P(),
        P(),
        P(("groups", "blk"), None),
        P(("groups", "blk"), None),
        P(("groups", "blk")),
    )
    return jax.shard_map(
        local,
        mesh=mesh,
        in_specs=placed,
        out_specs=P(None, None, ("groups", "blk")),
        check_vma=False,
    )
```

```python
import functools
import jax
import jax.numpy as jnp
from jax import lax
from jax.experimental import pallas as pl
from jax.experimental.pallas import tpu as pltpu
from jax.sharding import PartitionSpec as P

DOC_DEV = 32
STOPS = 12
NEWTON_STEPS = 6
LEAD = 5
TAIL = 16
F32 = jnp.float32
BF16 = jnp.bfloat16
HIGHEST_PRECISION = lax.Precision.HIGHEST
LAST_DIMS = (((1,), (1,)), ((), ()))


def pack_kernel(
    inputs_hbm, grads_hbm, pin_hbm, pout_hbm, owner_hbm, slot_hbm, send_ref, inputs_ref, grads_ref, pin_ref, pout_ref, owner_ref, slot_ref, sems
):
    owners, per, wide = send_ref.shape
    cap = per - TAIL
    toks, width = inputs_ref.shape
    low = pin_ref.shape[0]
    parts = sems.shape[1] - 1
    part = width // parts
    small = [
        pltpu.make_async_copy(owner_hbm, owner_ref, sems.at[0, parts]),
        pltpu.make_async_copy(slot_hbm, slot_ref, sems.at[1, parts]),
    ]
    large = []
    for i in range(parts):
        at = pl.ds(i * part, part)
        for j, (source, target) in enumerate(
            ((pin_hbm, pin_ref), (inputs_hbm, inputs_ref), (pout_hbm, pout_ref), (grads_hbm, grads_ref))
        ):
            large.append(pltpu.make_async_copy(source.at[:, at], target.at[:, at], sems.at[j, i]))
    for copy in small + large:
        copy.start()

    for copy in small:
        copy.wait()
    owner = owner_ref[...]
    hot = (owner == lax.broadcasted_iota(jnp.int32, (owners, toks), 0)).astype(F32)
    earlier = lax.broadcasted_iota(jnp.int32, (toks, toks), 0) < lax.broadcasted_iota(jnp.int32, (toks, toks), 1)
    before = jnp.dot(hot.astype(BF16), earlier.astype(F32).astype(BF16), preferred_element_type=F32)
    rank = jnp.sum(before * hot, axis=0, keepdims=True).astype(jnp.int32)
    position = owner * cap + rank
    placed = lax.broadcasted_iota(jnp.int32, (owners * cap, toks), 0) == position
    placed = placed.astype(F32).astype(BF16)
    named = (hot * (slot_ref[...].astype(F32) + 1.0)).astype(BF16)
    at_lane = lax.broadcasted_iota(jnp.int32, (wide, toks), 0) % cap == rank
    slots = lax.dot_general(named, at_lane.astype(F32).astype(BF16), LAST_DIMS, preferred_element_type=F32)
    for o in range(owners):
        send_ref[o, cap:, :] = jnp.broadcast_to(slots[o : o + 1], (TAIL, wide)).astype(BF16)

    inputs_low = jnp.zeros((toks, low), F32)
    grads_low = jnp.zeros((toks, low), F32)
    for i in range(parts):
        at = slice(i * part, (i + 1) * part)
        for copy in large[4 * i : 4 * i + 4]:
            copy.wait()
        inputs_low += lax.dot_general(inputs_ref[:, at], pin_ref[:, at], LAST_DIMS, preferred_element_type=F32)
        grads_low += lax.dot_general(grads_ref[:, at], pout_ref[:, at], LAST_DIMS, preferred_element_type=F32)
    both = jnp.concatenate([grads_low, inputs_low], axis=1).astype(BF16)
    rows = jnp.dot(placed, both, preferred_element_type=F32).astype(BF16)
    for o in range(owners):
        send_ref[o, :cap, :] = rows[o * cap : (o + 1) * cap]


def packed_rows(query_inputs, query_grads, proj_in, proj_out, token_owner, token_slot, owners, cap):
    toks, width = query_inputs.shape
    low = proj_in.shape[1]
    return pl.pallas_call(
        pack_kernel,
        out_shape=jax.ShapeDtypeStruct((owners, cap + TAIL, 2 * low), BF16),
        in_specs=[pl.BlockSpec(memory_space=pltpu.HBM)] * 6,
        out_specs=pl.BlockSpec(memory_space=pltpu.VMEM),
        scratch_shapes=[
            pltpu.VMEM((toks, width), BF16),
            pltpu.VMEM((toks, width), BF16),
            pltpu.VMEM((low, width), BF16),
            pltpu.VMEM((low, width), BF16),
            pltpu.VMEM((1, toks), jnp.int32),
            pltpu.VMEM((1, toks), jnp.int32),
            pltpu.SemaphoreType.DMA((4, 5)),
        ],
        compiler_params=pltpu.CompilerParams(vmem_limit_bytes=60 * 2**20),
    )(query_inputs, query_grads, proj_in.T, proj_out.T, token_owner.reshape(1, toks), token_slot.reshape(1, toks))


def split(value, parts):
    out = []
    for _ in range(parts):
        top = value.astype(BF16)
        out.append(top)
        value = value - top.astype(F32)
    return out


def times(left, right):
    rows = left.shape[0]
    parts = split(left, len(right))
    total = None
    for order, piece in enumerate(right):
        used = parts[: len(right) - order]
        got = jnp.dot(jnp.concatenate(used, axis=0), piece, preferred_element_type=F32)
        for j in range(len(used)):
            term = got[j * rows : (j + 1) * rows]
            total = term if total is None else total + term
    return total


def on_diagonal(wide, parts):
    rows = wide.shape[0]
    pair = wide.shape[1] // 2
    first = lax.broadcasted_iota(jnp.int32, (rows, pair), 1) < rows
    zero = jnp.zeros((rows, pair), BF16)
    out = []
    for part in split(wide, parts):
        ahead, after = part[:, :pair], part[:, pair:]
        none = jnp.zeros_like(ahead)
        out.append(
            jnp.concatenate(
                [
                    jnp.concatenate([jnp.where(first, ahead, none), zero], axis=1),
                    jnp.concatenate([jnp.where(first, none, ahead), zero], axis=1),
                    jnp.concatenate([zero, jnp.where(first, after, none)], axis=1),
                    jnp.concatenate([zero, jnp.where(first, none, after)], axis=1),
                ],
                axis=0,
            )
        )
    return out


def query_kernel(first_doc, recv_ref, out_ref, gram_ref, rows_ref, count_ref):
    docs, low, _ = out_ref.shape
    sources, per, wide = recv_ref.shape
    cap = per - TAIL
    rows = jnp.concatenate([recv_ref[s, :cap, :] for s in range(sources)], axis=0)
    rows_ref[...] = rows.T
    half = lax.broadcasted_iota(jnp.int32, (1, wide), 1) < low
    named = [recv_ref[s, cap:, :].astype(F32)[:1] for s in range(sources)]
    slot = jnp.concatenate([jnp.where(half, named[s], named[s + 1]) for s in range(0, sources, 2)], axis=1)
    across = rows_ref[...]
    for d in range(docs):
        mine = (slot == (first_doc + d + 1)).astype(F32)
        gram_ref[d] = jnp.dot(across * mine.astype(BF16), rows, preferred_element_type=F32)
        count_ref[d : d + 1, :] = jnp.broadcast_to(jnp.sum(mine, axis=1, keepdims=True), (1, wide))

    row_at = lax.broadcasted_iota(jnp.int32, (low, wide), 0)
    lane_at = lax.broadcasted_iota(jnp.int32, (low, wide), 1)
    first = lane_at < low
    eye = ((row_at == lane_at) | (row_at + low == lane_at)).astype(F32)
    eyes = jnp.concatenate([eye, eye], axis=1)
    powers, scales, mixed = [], [], []
    for g in range(0, docs, 2):
        errors, inverses, grads = [], [], []
        for d in (g, g + 1):
            both = gram_ref[d]
            outer = jnp.where(first, both[:low], both[low:])
            damped = outer / (count_ref[d : d + 1, :] + 1.0) + eye
            sums = jnp.sum(jnp.abs(damped), axis=0, keepdims=True)
            bound_b = jnp.max(jnp.where(half, sums, 0.0), axis=1, keepdims=True)
            bound_a = jnp.max(jnp.where(half, 0.0, sums), axis=1, keepdims=True)
            inverse = 1.0 / jnp.where(half, bound_b, bound_a)
            errors.append(eye - damped * inverse)
            inverses.append(inverse)
            grads.append(jnp.where(first, 0.0, both[:low]))
        powers.append(jnp.concatenate(errors, axis=1))
        scales.append(jnp.concatenate(inverses, axis=1))
        mixed.append(grads)
    totals = [eyes + power for power in powers]
    powers = [times(power, on_diagonal(power, 2)) for power in powers]
    for _ in range(NEWTON_STEPS - 2):
        stepped = [
            times(jnp.concatenate([power, total], axis=0), on_diagonal(power, 2))
            for power, total in zip(powers, totals)
        ]
        powers = [both[:low] for both in stepped]
        totals = [total + both[low:] for total, both in zip(totals, stepped)]
    totals = [total + times(total, on_diagonal(power, 2)) for power, total in zip(powers, totals)]
    totals = [total * scale for total, scale in zip(totals, scales)]
    tilted = []
    for total, grads in zip(totals, mixed):
        right = []
        gap = jnp.zeros((low, 2 * wide), BF16)
        zero = jnp.zeros((low, wide), BF16)
        for ahead, after in zip(split(grads[0], 3), split(grads[1], 3)):
            right.append(
                jnp.concatenate(
                    [jnp.concatenate([ahead, zero], axis=1), gap, jnp.concatenate([zero, after], axis=1), gap], axis=0
                )
            )
        tilted.append(times(total, right))
    found = [times(tilt, on_diagonal(total, 3)) for tilt, total in zip(tilted, totals)]
    for g, query in enumerate(found):
        out_ref[2 * g] = query[:, low:wide].astype(BF16)
        out_ref[2 * g + 1] = query[:, wide + low :].astype(BF16)


def queries_of(recv, first_doc, docs, low):
    sources, per, wide = recv.shape
    found = pl.pallas_call(
        functools.partial(query_kernel, first_doc),
        out_shape=jax.ShapeDtypeStruct((docs, low, low), BF16),
        in_specs=[pl.BlockSpec(memory_space=pltpu.VMEM)],
        out_specs=pl.BlockSpec(memory_space=pltpu.VMEM),
        scratch_shapes=[
            pltpu.VMEM((docs, wide, wide), F32),
            pltpu.VMEM((wide, sources * (per - TAIL)), BF16),
            pltpu.VMEM((docs, wide), F32),
        ],
        cost_estimate=pl.CostEstimate(flops=4 * 10**9, bytes_accessed=2**20, transcendentals=0),
        compiler_params=pltpu.CompilerParams(vmem_limit_bytes=16 * 2**20),
    )(recv)
    return found.reshape(docs, low * low)


def score_kernel(*refs):
    own_rows, other_rows, own_ref, other_ref = refs[-4:]
    blocks = jnp.concatenate([ref[...] for ref in refs[:-4]], axis=0)
    own_ref[...] = lax.dot_general(blocks, own_rows[...], LAST_DIMS, preferred_element_type=F32).astype(BF16)
    other_ref[...] = lax.dot_general(blocks, other_rows[...], LAST_DIMS, preferred_element_type=F32).astype(BF16)


def scores_of(blocks, own_rows, other_rows):
    count = sum(block.shape[0] for block in blocks)
    shape = jax.ShapeDtypeStruct((count, own_rows.shape[0]), BF16)
    return pl.pallas_call(
        score_kernel,
        out_shape=(shape, shape),
        in_specs=[pl.BlockSpec(memory_space=pltpu.VMEM)] * (len(blocks) + 2),
        out_specs=(pl.BlockSpec(memory_space=pltpu.VMEM),) * 2,
        cost_estimate=pl.CostEstimate(flops=1, bytes_accessed=1, transcendentals=0),
        compiler_params=pltpu.CompilerParams(vmem_limit_bytes=16 * 2**20),
    )(*blocks, own_rows, other_rows)


def order_kernel(owners, docs, places, *refs):
    out_ref, sems = refs[-2:]
    chips = owners // 2
    device = lax.axis_index("blk")
    chip, core = lax.div(device, 2), lax.rem(device, 2)
    spot = jnp.where(lax.rem(chip, 2) == 0, lax.div(chip, 2), chips - 1 - lax.div(chip, 2))
    copies = []
    for ref, (own, listed) in zip(refs, places):
        scorer = core if own else 1 - core
        for number, (chunk, hop, second) in enumerate(listed):
            there = lax.rem(spot + jnp.where(scorer == 0, chips - hop, hop), chips)
            where = jnp.where(there < chips // 2, 2 * there, 2 * (chips - 1 - there) + 1)
            owner = 2 * where + (scorer if hop in (0, chips // 2) else second)
            stop = lax.rem(device + LEAD - owner + owners, owners)
            wanted = stop < out_ref.shape[0]
            copy = pltpu.make_async_copy(
                ref.at[pl.ds(number * docs, docs), :],
                out_ref.at[jnp.minimum(stop, out_ref.shape[0] - 1), pl.ds(chunk * docs, docs), :],
                sems.at[len(copies)],
            )
            copies.append((wanted, copy))
            pl.when(wanted)(copy.start)
    for wanted, copy in copies:
        pl.when(wanted)(copy.wait)


def put_in_order(tiles, owners, docs, placed):
    refs = [ref for ref, _, _ in tiles]
    places = [(own, listing) for _, own, listing in tiles]
    shape = jax.ShapeDtypeStruct((STOPS, DOC_DEV, refs[0].shape[1]), BF16)
    kernel = functools.partial(order_kernel, owners, docs, places)
    aliases = {}
    if placed is not None:
        aliases = {len(refs): 0}
        refs = refs + [placed]
    specs = [pl.BlockSpec(memory_space=pltpu.VMEM)] * len(tiles) + [pl.BlockSpec(memory_space=pltpu.HBM)] * len(aliases)
    if aliases:
        inner = kernel

        def kernel(*args):
            inner(*args[: len(tiles)], *args[len(tiles) + 1 :])

    return pl.pallas_call(
        kernel,
        out_shape=shape,
        in_specs=specs,
        out_specs=pl.BlockSpec(memory_space=pltpu.HBM),
        input_output_aliases=aliases,
        scratch_shapes=[pltpu.SemaphoreType.DMA((sum(len(listing) for _, _, listing in tiles),))],
        cost_estimate=pl.CostEstimate(flops=1, bytes_accessed=1, transcendentals=0),
        compiler_params=pltpu.CompilerParams(vmem_limit_bytes=4 * 2**20),
    )(*refs)


def ring_pairs(owners):
    chips = owners // 2
    line = chips // 2
    chip_at = [2 * p if p < line else 2 * (chips - 1 - p) + 1 for p in range(chips)]
    pairs = []
    for p in range(chips):
        pairs.append((2 * chip_at[p], 2 * chip_at[(p + 1) % chips]))
        pairs.append((2 * chip_at[p] + 1, 2 * chip_at[(p - 1) % chips] + 1))
    return pairs, [(device, device ^ 1) for device in range(owners)]


def gathered(query_inputs, query_grads, proj_in, proj_out, train_rows, token_owner, token_slot):
    toks = query_inputs.shape[0]
    low = proj_in.shape[1]
    owners = lax.axis_size("blk")
    hops = owners // 4
    train = train_rows.shape[0]
    cap = 4 * toks // owners
    docs = DOC_DEV // 2
    ring, swap = ring_pairs(owners)
    odd = lax.rem(lax.axis_index("blk"), 2) == 1

    send = packed_rows(query_inputs, query_grads, proj_in, proj_out, token_owner, token_slot, owners, cap)
    other_rows = lax.ppermute(train_rows, "blk", swap)
    recv = lax.all_to_all(send, "blk", split_axis=0, concat_axis=0, tiled=True)
    recv, other_rows = lax.optimization_barrier((recv, other_rows))

    def pair_up(mine):
        theirs = lax.ppermute(mine, "blk", swap)
        return jnp.concatenate([jnp.where(odd, theirs, mine), jnp.where(odd, mine, theirs)], axis=0)

    def onward(block, hop):
        if hop == hops:
            block = jnp.where(odd, block[docs:], block[:docs])
        return lax.ppermute(block, "blk", ring)

    def listed(chunk, hop):
        return [(chunk, hop, second) for second in ((0,) if hop in (0, hops) else (0, 1))]

    first_own = queries_of(recv, 0, docs, low)
    first = pair_up(first_own)
    recv, first = lax.optimization_barrier((recv, first))
    last_own = queries_of(recv, docs, docs, low)
    first = onward(first, 1)
    last_own, first = lax.optimization_barrier((last_own, first))
    last = pair_up(last_own)
    waiting = [first_own, last_own, first]
    lists = listed(0, 0) + listed(1, 0) + listed(0, 1)
    scored, places = [], []
    for hop in range(1, hops + 1):
        ahead = onward(first, hop + 1) if hop < hops else None
        came = onward(last, hop)
        scored.append(scores_of(waiting, train_rows, other_rows))
        places.append(lists)
        if hop < hops - 1:
            ahead, scored[-1] = lax.optimization_barrier((ahead, scored[-1]))
        elif hop == hops - 1:
            came, scored[-1] = lax.optimization_barrier((came, scored[-1]))
        waiting = [came] if ahead is None else [ahead, came]
        lists = ([] if ahead is None else listed(0, hop + 1)) + listed(1, hop)
        first, last = ahead, came
    early = lax.ppermute(jnp.concatenate([other for _, other in scored], axis=0), "blk", swap)
    final = scores_of(waiting, train_rows, other_rows)
    late = lax.ppermute(final[1], "blk", swap)
    most = [(own, True, listing) for (own, _), listing in zip(scored, places)] + [(early, False, sum(places, []))]
    placed = put_in_order(most, owners, docs, None)
    return put_in_order([(final[0], True, lists), (late, False, lists)], owners, docs, placed)


def passed_along(value, axis, steps):
    count = lax.axis_size(axis)
    pairs = [(source, (source + steps) % count) for source in range(count)]
    return lax.ppermute(value, axis, pairs)


def inverse_factor(gram_sum, counts):
    width_low = gram_sum.shape[1]
    identity_mat = jnp.eye(width_low, dtype=jnp.float32)
    damped = gram_sum / (counts[:, None, None] + 1.0) + identity_mat[None]
    row_bound = jnp.max(jnp.sum(jnp.abs(damped), axis=2), axis=1)
    approx = identity_mat[None] / row_bound[:, None, None]
    for iteration in range(NEWTON_STEPS):
        product = jnp.einsum("dab,dbc->dac", damped, approx, precision=HIGHEST_PRECISION)
        approx = jnp.einsum(
            "dab,dbc->dac", approx, 2.0 * identity_mat[None] - product, precision=HIGHEST_PRECISION
        )
    return approx


def passed(query_inputs, query_grads, proj_in, proj_out, train_rows, token_owner, token_slot):
    tok_count = query_inputs.shape[0]
    width_low = proj_in.shape[1]
    owners = lax.axis_size("blk")
    capacity = 4 * tok_count // owners
    grads_low = jnp.dot(query_grads, proj_out, preferred_element_type=jnp.float32).astype(
        jnp.bfloat16
    )
    inputs_low = jnp.dot(query_inputs, proj_in, preferred_element_type=jnp.float32).astype(
        jnp.bfloat16
    )
    low_rows = jnp.concatenate([grads_low, inputs_low], axis=1)
    owner_ids = token_owner[:, 0]
    owner_hot = (owner_ids[:, None] == jnp.arange(owners, dtype=jnp.int32)[None, :]).astype(
        jnp.float32
    )
    tok_index = jnp.arange(tok_count, dtype=jnp.int32)
    earlier = (tok_index[:, None] > tok_index[None, :]).astype(jnp.float32)
    before = jnp.dot(earlier, owner_hot, precision=HIGHEST_PRECISION)
    rank_in = jnp.sum(before * owner_hot, axis=1).astype(jnp.int32)
    position = owner_ids * capacity + rank_in
    slot_index = jnp.arange(owners * capacity, dtype=jnp.int32)
    placed = slot_index[:, None] == position[None, :]
    send_rows = jnp.dot(
        placed.astype(jnp.bfloat16), low_rows, preferred_element_type=jnp.float32
    ).astype(jnp.bfloat16)
    send_slot = jnp.sum(jnp.where(placed, token_slot[None, :] + 1, 0), axis=1)
    recv_rows, recv_slot = (
        lax.all_to_all(
            send_rows.reshape(owners, capacity, 2 * width_low),
            "blk",
            split_axis=0,
            concat_axis=0,
            tiled=True,
        ),
        lax.all_to_all(
            send_slot.reshape(owners, capacity), "blk", split_axis=0, concat_axis=0, tiled=True
        ),
    )
    recv_rows = recv_rows.reshape(owners * capacity, 2 * width_low)
    recv_slot = recv_slot.reshape(owners * capacity)
    doc_index = jnp.arange(1, DOC_DEV + 1, dtype=jnp.int32)
    doc_hot = recv_slot[:, None] == doc_index[None, :]
    counts = jnp.sum(doc_hot.astype(jnp.float32), axis=0)
    hot_bf = doc_hot.astype(jnp.bfloat16)
    grads_recv = recv_rows[:, :width_low]
    inputs_recv = recv_rows[:, width_low:]
    spread_grads = (hot_bf[:, :, None] * grads_recv[:, None, :]).reshape(
        owners * capacity, DOC_DEV * width_low
    )
    spread_inputs = (hot_bf[:, :, None] * inputs_recv[:, None, :]).reshape(
        owners * capacity, DOC_DEV * width_low
    )
    contract = (((0,), (0,)), ((), ()))
    grad_gram = lax.dot_general(
        spread_grads, recv_rows, contract, preferred_element_type=jnp.float32
    ).reshape(DOC_DEV, width_low, 2 * width_low)
    outer_b = grad_gram[:, :, :width_low]
    doc_grad = grad_gram[:, :, width_low:]
    outer_a = lax.dot_general(
        spread_inputs, inputs_recv, contract, preferred_element_type=jnp.float32
    ).reshape(DOC_DEV, width_low, width_low)
    inv_a = inverse_factor(outer_a, counts)
    inv_b = inverse_factor(outer_b, counts)
    tilted = jnp.einsum("dab,dbc->dac", inv_b, doc_grad, precision=HIGHEST_PRECISION)
    tilted = jnp.einsum("dab,dbc->dac", tilted, inv_a, precision=HIGHEST_PRECISION)
    queries = tilted.reshape(DOC_DEV, width_low * width_low).astype(jnp.bfloat16)
    score_dims = (((1,), (1,)), ((), ()))

    def scoring(block):
        return lax.dot_general(
            block, train_rows, score_dims, preferred_element_type=jnp.float32
        ).astype(jnp.bfloat16)

    def step_ahead(current_block, unused):
        arrived = passed_along(current_block, "blk", 1)
        return (arrived, scoring(arrived))

    def step_back(current_block):
        arrived = passed_along(current_block, "blk", -1)
        return (arrived, scoring(arrived))

    def both_ways(carried, unused):
        ahead_block, back_block = carried
        ahead_block, ahead_tile = step_ahead(ahead_block, unused)
        back_block, back_tile = step_back(back_block)
        return ((ahead_block, back_block), (ahead_tile, back_tile))

    last_pair, paired_tiles = lax.scan(both_ways, (queries, queries), None, length=LEAD)
    ahead_tiles, back_tiles = paired_tiles
    tail_block, tail_tiles = lax.scan(step_ahead, last_pair[0], None, length=STOPS - 1 - 2 * LEAD)
    stacked = jnp.concatenate(
        [jnp.flip(back_tiles, 0), scoring(queries)[None], ahead_tiles, tail_tiles], axis=0
    )
    return stacked


def solution(mesh):
    owners = mesh.shape["blk"]

    def local(query_inputs, query_grads, proj_in, *rest):
        low = proj_in.shape[1]
        cap = 4 * query_inputs.shape[0] // owners
        close = owners % 4 == 0 and STOPS <= owners <= 2 * STOPS and cap == low and cap % TAIL == 0
        return (gathered if close else passed)(query_inputs, query_grads, proj_in, *rest)

    placed = (
        P(("groups", "blk"), None),
        P(("groups", "blk"), None),
        P(),
        P(),
        P(("groups", "blk"), None),
        P(("groups", "blk"), None),
        P(("groups", "blk")),
    )
    return jax.shard_map(
        local,
        mesh=mesh,
        in_specs=placed,
        out_specs=P(None, None, ("groups", "blk")),
        check_vma=False,
    )
```

```python
import functools
import jax
import jax.numpy as jnp
from jax import lax
from jax.experimental import pallas as pl
from jax.experimental.pallas import tpu as pltpu
from jax.sharding import PartitionSpec as P

DOC_DEV = 32
STOPS = 12
NEWTON_STEPS = 6
LEAD = 5
TAIL = 16
GRAM_DOCS = 2
SCORE_COST = 6 * 10**9
F32 = jnp.float32
BF16 = jnp.bfloat16
HIGHEST_PRECISION = lax.Precision.HIGHEST
LAST_DIMS = (((1,), (1,)), ((), ()))


def pack_kernel(
    inputs_hbm, grads_hbm, pin_hbm, pout_hbm, owner_hbm, slot_hbm, send_ref, inputs_ref, grads_ref, pin_ref, pout_ref, owner_ref, slot_ref, sems
):
    owners, per, wide = send_ref.shape
    cap = per - TAIL
    toks, width = inputs_ref.shape
    low = pin_ref.shape[0]
    parts = sems.shape[1] - 1
    part = width // parts
    small = [
        pltpu.make_async_copy(owner_hbm, owner_ref, sems.at[0, parts]),
        pltpu.make_async_copy(slot_hbm, slot_ref, sems.at[1, parts]),
    ]
    large = []
    for i in range(parts):
        at = pl.ds(i * part, part)
        for j, (source, target) in enumerate(
            ((pin_hbm, pin_ref), (inputs_hbm, inputs_ref), (pout_hbm, pout_ref), (grads_hbm, grads_ref))
        ):
            large.append(pltpu.make_async_copy(source.at[:, at], target.at[:, at], sems.at[j, i]))
    for copy in small + large:
        copy.start()

    for copy in small:
        copy.wait()
    owner = owner_ref[...]
    hot = (owner == lax.broadcasted_iota(jnp.int32, (owners, toks), 0)).astype(F32)
    earlier = lax.broadcasted_iota(jnp.int32, (toks, toks), 0) < lax.broadcasted_iota(jnp.int32, (toks, toks), 1)
    before = jnp.dot(hot.astype(BF16), earlier.astype(F32).astype(BF16), preferred_element_type=F32)
    rank = jnp.sum(before * hot, axis=0, keepdims=True).astype(jnp.int32)
    position = owner * cap + rank
    placed = lax.broadcasted_iota(jnp.int32, (owners * cap, toks), 0) == position
    placed = placed.astype(F32).astype(BF16)
    named = (hot * (slot_ref[...].astype(F32) + 1.0)).astype(BF16)
    at_lane = lax.broadcasted_iota(jnp.int32, (wide, toks), 0) % cap == rank
    slots = lax.dot_general(named, at_lane.astype(F32).astype(BF16), LAST_DIMS, preferred_element_type=F32)
    for o in range(owners):
        send_ref[o, cap:, :] = jnp.broadcast_to(slots[o : o + 1], (TAIL, wide)).astype(BF16)

    inputs_low = jnp.zeros((toks, low), F32)
    grads_low = jnp.zeros((toks, low), F32)
    for i in range(parts):
        at = slice(i * part, (i + 1) * part)
        for copy in large[4 * i : 4 * i + 4]:
            copy.wait()
        inputs_low += lax.dot_general(inputs_ref[:, at], pin_ref[:, at], LAST_DIMS, preferred_element_type=F32)
        grads_low += lax.dot_general(grads_ref[:, at], pout_ref[:, at], LAST_DIMS, preferred_element_type=F32)
    both = jnp.concatenate([grads_low, inputs_low], axis=1).astype(BF16)
    rows = jnp.dot(placed, both, preferred_element_type=F32).astype(BF16)
    for o in range(owners):
        send_ref[o, :cap, :] = rows[o * cap : (o + 1) * cap]


def packed_rows(query_inputs, query_grads, proj_in, proj_out, token_owner, token_slot, owners, cap):
    toks, width = query_inputs.shape
    low = proj_in.shape[1]
    return pl.pallas_call(
        pack_kernel,
        out_shape=jax.ShapeDtypeStruct((owners, cap + TAIL, 2 * low), BF16),
        in_specs=[pl.BlockSpec(memory_space=pltpu.HBM)] * 6,
        out_specs=pl.BlockSpec(memory_space=pltpu.VMEM),
        scratch_shapes=[
            pltpu.VMEM((toks, width), BF16),
            pltpu.VMEM((toks, width), BF16),
            pltpu.VMEM((low, width), BF16),
            pltpu.VMEM((low, width), BF16),
            pltpu.VMEM((1, toks), jnp.int32),
            pltpu.VMEM((1, toks), jnp.int32),
            pltpu.SemaphoreType.DMA((4, 5)),
        ],
        compiler_params=pltpu.CompilerParams(vmem_limit_bytes=60 * 2**20),
    )(query_inputs, query_grads, proj_in.T, proj_out.T, token_owner.reshape(1, toks), token_slot.reshape(1, toks))


def split(value, parts):
    out = []
    for _ in range(parts):
        top = value.astype(BF16)
        out.append(top)
        value = value - top.astype(F32)
    return out


def times(left, right):
    rows = left.shape[0]
    parts = split(left, len(right))
    total = None
    for order, piece in enumerate(right):
        used = parts[: len(right) - order]
        got = jnp.dot(jnp.concatenate(used, axis=0), piece, preferred_element_type=F32)
        for j in range(len(used)):
            term = got[j * rows : (j + 1) * rows]
            total = term if total is None else total + term
    return total


def on_diagonal(wide, parts):
    rows = wide.shape[0]
    pair = wide.shape[1] // 2
    first = lax.broadcasted_iota(jnp.int32, (rows, pair), 1) < rows
    zero = jnp.zeros((rows, pair), BF16)
    out = []
    for part in split(wide, parts):
        ahead, after = part[:, :pair], part[:, pair:]
        none = jnp.zeros_like(ahead)
        out.append(
            jnp.concatenate(
                [
                    jnp.concatenate([jnp.where(first, ahead, none), zero], axis=1),
                    jnp.concatenate([jnp.where(first, none, ahead), zero], axis=1),
                    jnp.concatenate([zero, jnp.where(first, after, none)], axis=1),
                    jnp.concatenate([zero, jnp.where(first, none, after)], axis=1),
                ],
                axis=0,
            )
        )
    return out


def query_kernel(first_doc, recv_ref, out_ref, gram_ref, rows_ref, count_ref):
    docs, low, _ = out_ref.shape
    sources, per, wide = recv_ref.shape
    cap = per - TAIL
    rows = jnp.concatenate([recv_ref[s, :cap, :] for s in range(sources)], axis=0)
    rows_ref[...] = rows.T
    half = lax.broadcasted_iota(jnp.int32, (1, wide), 1) < low
    named = [recv_ref[s, cap:, :].astype(F32)[:1] for s in range(sources)]
    slot = jnp.concatenate([jnp.where(half, named[s], named[s + 1]) for s in range(0, sources, 2)], axis=1)
    across = rows_ref[...]
    for d in range(0, docs, GRAM_DOCS):
        picked = []
        for e in range(d, d + GRAM_DOCS):
            mine = (slot == (first_doc + e + 1)).astype(F32)
            picked.append(across * mine.astype(BF16))
            count_ref[e : e + 1, :] = jnp.broadcast_to(jnp.sum(mine, axis=1, keepdims=True), (1, wide))
        gram = jnp.dot(jnp.concatenate(picked, axis=0), rows, preferred_element_type=F32)
        gram_ref[d : d + GRAM_DOCS] = gram.reshape(GRAM_DOCS, wide, wide)

    row_at = lax.broadcasted_iota(jnp.int32, (low, wide), 0)
    lane_at = lax.broadcasted_iota(jnp.int32, (low, wide), 1)
    first = lane_at < low
    eye = ((row_at == lane_at) | (row_at + low == lane_at)).astype(F32)
    eyes = jnp.concatenate([eye, eye], axis=1)
    powers, scales, mixed = [], [], []
    for g in range(0, docs, 2):
        errors, inverses, grads = [], [], []
        for d in (g, g + 1):
            both = gram_ref[d]
            outer = jnp.where(first, both[:low], both[low:])
            damped = outer / (count_ref[d : d + 1, :] + 1.0) + eye
            sums = jnp.sum(jnp.abs(damped), axis=0, keepdims=True)
            bound_b = jnp.max(jnp.where(half, sums, 0.0), axis=1, keepdims=True)
            bound_a = jnp.max(jnp.where(half, 0.0, sums), axis=1, keepdims=True)
            inverse = 1.0 / jnp.where(half, bound_b, bound_a)
            errors.append(eye - damped * inverse)
            inverses.append(inverse)
            grads.append(jnp.where(first, 0.0, both[:low]))
        powers.append(jnp.concatenate(errors, axis=1))
        scales.append(jnp.concatenate(inverses, axis=1))
        mixed.append(grads)
    totals = [eyes + power for power in powers]
    powers = [times(power, on_diagonal(power, 2)) for power in powers]
    for _ in range(NEWTON_STEPS - 2):
        stepped = [
            times(jnp.concatenate([power, total], axis=0), on_diagonal(power, 2))
            for power, total in zip(powers, totals)
        ]
        powers = [both[:low] for both in stepped]
        totals = [total + both[low:] for total, both in zip(totals, stepped)]
    totals = [total + times(total, on_diagonal(power, 2)) for power, total in zip(powers, totals)]
    totals = [total * scale for total, scale in zip(totals, scales)]
    tilted = []
    for total, grads in zip(totals, mixed):
        right = []
        gap = jnp.zeros((low, 2 * wide), BF16)
        zero = jnp.zeros((low, wide), BF16)
        for ahead, after in zip(split(grads[0], 3), split(grads[1], 3)):
            right.append(
                jnp.concatenate(
                    [jnp.concatenate([ahead, zero], axis=1), gap, jnp.concatenate([zero, after], axis=1), gap], axis=0
                )
            )
        tilted.append(times(total, right))
    found = [times(tilt, on_diagonal(total, 3)) for tilt, total in zip(tilted, totals)]
    for g, query in enumerate(found):
        out_ref[2 * g] = query[:, low:wide].astype(BF16)
        out_ref[2 * g + 1] = query[:, wide + low :].astype(BF16)


def queries_of(recv, first_doc, docs, low):
    sources, per, wide = recv.shape
    found = pl.pallas_call(
        functools.partial(query_kernel, first_doc),
        out_shape=jax.ShapeDtypeStruct((docs, low, low), BF16),
        in_specs=[pl.BlockSpec(memory_space=pltpu.VMEM)],
        out_specs=pl.BlockSpec(memory_space=pltpu.VMEM),
        scratch_shapes=[
            pltpu.VMEM((docs, wide, wide), F32),
            pltpu.VMEM((wide, sources * (per - TAIL)), BF16),
            pltpu.VMEM((docs, wide), F32),
        ],
        cost_estimate=pl.CostEstimate(flops=4 * 10**9, bytes_accessed=2**20, transcendentals=0),
        compiler_params=pltpu.CompilerParams(vmem_limit_bytes=16 * 2**20),
    )(recv)
    return found.reshape(docs, low * low)


def score_kernel(*refs):
    own_rows, other_rows, own_ref, other_ref = refs[-4:]
    blocks = jnp.concatenate([ref[...] for ref in refs[:-4]], axis=0)
    own_ref[...] = lax.dot_general(blocks, own_rows[...], LAST_DIMS, preferred_element_type=F32).astype(BF16)
    other_ref[...] = lax.dot_general(blocks, other_rows[...], LAST_DIMS, preferred_element_type=F32).astype(BF16)


def bring_and_score_kernel(*refs):
    own_rows, other_hbm, own_ref, other_ref, kept_ref, sems = refs[-6:]
    parts = sems.shape[0]
    part = kept_ref.shape[1] // parts
    places = [slice(i * part, (i + 1) * part) for i in range(parts)]
    copies = [
        pltpu.make_async_copy(other_hbm.at[:, pl.ds(i * part, part)], kept_ref.at[:, pl.ds(i * part, part)], sems.at[i])
        for i in range(parts)
    ]
    for copy in copies:
        copy.start()
    blocks = jnp.concatenate([ref[...] for ref in refs[:-6]], axis=0)
    own_ref[...] = lax.dot_general(blocks, own_rows[...], LAST_DIMS, preferred_element_type=F32).astype(BF16)
    total = jnp.zeros(other_ref.shape, F32)
    for at, copy in zip(places, copies):
        copy.wait()
        total += lax.dot_general(blocks[:, at], kept_ref[:, at], LAST_DIMS, preferred_element_type=F32)
    other_ref[...] = total.astype(BF16)


def scores_of(blocks, own_rows, other_rows, bring):
    count = sum(block.shape[0] for block in blocks)
    shape = jax.ShapeDtypeStruct((count, own_rows.shape[0]), BF16)
    vmem = pl.BlockSpec(memory_space=pltpu.VMEM)
    kept = [jax.ShapeDtypeStruct(other_rows.shape, BF16)] if bring else []
    return pl.pallas_call(
        bring_and_score_kernel if bring else score_kernel,
        out_shape=[shape, shape] + kept,
        in_specs=[vmem] * (len(blocks) + 1) + [pl.BlockSpec(memory_space=pltpu.HBM) if bring else vmem],
        out_specs=[vmem] * (2 + len(kept)),
        scratch_shapes=[pltpu.SemaphoreType.DMA((4,))] if bring else [],
        cost_estimate=pl.CostEstimate(flops=SCORE_COST, bytes_accessed=2**20, transcendentals=0),
        compiler_params=pltpu.CompilerParams(vmem_limit_bytes=16 * 2**20),
    )(*blocks, own_rows, other_rows)


def order_kernel(owners, docs, places, *refs):
    out_ref, sems = refs[-2:]
    chips = owners // 2
    device = lax.axis_index("blk")
    chip, core = lax.div(device, 2), lax.rem(device, 2)
    spot = jnp.where(lax.rem(chip, 2) == 0, lax.div(chip, 2), chips - 1 - lax.div(chip, 2))
    copies = []
    for ref, (own, listed) in zip(refs, places):
        scorer = core if own else 1 - core
        for number, (chunk, hop, partner) in enumerate(listed):
            there = lax.rem(spot + jnp.where(scorer == 0, chips - hop, hop), chips)
            where = jnp.where(there < chips // 2, 2 * there, 2 * (chips - 1 - there) + 1)
            owner = 2 * where + (1 - scorer if partner else scorer)
            stop = lax.rem(device + LEAD - owner + owners, owners)
            wanted = stop < out_ref.shape[0]
            copy = pltpu.make_async_copy(
                ref.at[pl.ds(number * docs, docs), :],
                out_ref.at[jnp.minimum(stop, out_ref.shape[0] - 1), pl.ds(chunk * docs, docs), :],
                sems.at[len(copies)],
            )
            copies.append((wanted, copy))
            pl.when(wanted)(copy.start)
    for wanted, copy in copies:
        pl.when(wanted)(copy.wait)


def put_in_order(tiles, owners, docs, placed):
    refs = [ref for ref, _, _ in tiles]
    places = [(own, listing) for _, own, listing in tiles]
    shape = jax.ShapeDtypeStruct((STOPS, DOC_DEV, refs[0].shape[1]), BF16)
    kernel = functools.partial(order_kernel, owners, docs, places)
    aliases = {}
    if placed is not None:
        aliases = {len(refs): 0}
        refs = refs + [placed]
    specs = [pl.BlockSpec(memory_space=pltpu.VMEM)] * len(tiles) + [pl.BlockSpec(memory_space=pltpu.HBM)] * len(aliases)
    if aliases:
        inner = kernel

        def kernel(*args):
            inner(*args[: len(tiles)], *args[len(tiles) + 1 :])

    return pl.pallas_call(
        kernel,
        out_shape=shape,
        in_specs=specs,
        out_specs=pl.BlockSpec(memory_space=pltpu.HBM),
        input_output_aliases=aliases,
        scratch_shapes=[pltpu.SemaphoreType.DMA((sum(len(listing) for _, _, listing in tiles),))],
        cost_estimate=pl.CostEstimate(flops=1, bytes_accessed=1, transcendentals=0),
        compiler_params=pltpu.CompilerParams(vmem_limit_bytes=4 * 2**20),
    )(*refs)


def ring_pairs(owners):
    chips = owners // 2
    line = chips // 2
    chip_at = [2 * p if p < line else 2 * (chips - 1 - p) + 1 for p in range(chips)]
    pairs = []
    for p in range(chips):
        pairs.append((2 * chip_at[p], 2 * chip_at[(p + 1) % chips]))
        pairs.append((2 * chip_at[p] + 1, 2 * chip_at[(p - 1) % chips] + 1))
    return pairs, [(device, device ^ 1) for device in range(owners)]


def gathered(query_inputs, query_grads, proj_in, proj_out, train_rows, token_owner, token_slot):
    toks = query_inputs.shape[0]
    low = proj_in.shape[1]
    owners = lax.axis_size("blk")
    hops = owners // 4
    train = train_rows.shape[0]
    cap = 4 * toks // owners
    docs = DOC_DEV // 2
    ring, swap = ring_pairs(owners)

    send = packed_rows(query_inputs, query_grads, proj_in, proj_out, token_owner, token_slot, owners, cap)
    recv = lax.all_to_all(send, "blk", split_axis=0, concat_axis=0, tiled=True)

    def ring_on(block, links=ring):
        return lax.ppermute(block, "blk", links)

    following = dict(ring)
    second_next = [(device, following[step]) for device, step in ring]

    first_own = queries_of(recv, 0, docs, low)
    first_next, first_second = ring_on(first_own), ring_on(first_own, second_next)
    first_given = lax.ppermute(first_own, "blk", swap)
    recv, train_rows, first_own = lax.optimization_barrier((recv, train_rows, first_own))
    other_rows = lax.ppermute(train_rows, "blk", swap)
    last_own = queries_of(recv, docs, docs, low)
    last_own, first_next, first_second, first_given = lax.optimization_barrier(
        (last_own, first_next, first_second, first_given)
    )
    waiting = [first_own, last_own, first_next, first_second]
    lists = [(0, 0, 0), (1, 0, 0), (0, 1, 0), (0, 2, 0)]
    first = jnp.concatenate([first_second, first_given], axis=0)
    last = jnp.concatenate([last_own, lax.ppermute(last_own, "blk", swap)], axis=0)
    for hop in range(1, hops):
        near = hop < hops - 1
        first = ring_on(first if near else first[docs:])
        if near:
            waiting.append(first)
            lists = lists + [(0, hop + 2, 0), (0, hop, 1)]
        else:
            most, most_lists, waiting, lists = waiting, lists, before, before_lists
            waiting = waiting + [first]
            lists = lists + [(0, hop, 1)]
        last = ring_on(last)
        came, listed = [last], [(1, hop + 1, 0), (1, hop, 1)]
        if hop == 1:
            last_second = ring_on(last_own, second_next)
            came, listed = [last, last_second], [(1, 1, 0), (1, 1, 1), (1, 2, 0)]
            last = jnp.concatenate([last_second, last[docs:]], axis=0)
        if hop == hops - 2:
            before, before_lists = came, listed
        else:
            waiting = waiting + came
            lists = lists + listed
    own_most, other_most, other_rows = scores_of(most, train_rows, other_rows, True)
    early = lax.ppermute(other_most, "blk", swap)
    own_late, other_late = scores_of(waiting, train_rows, other_rows, False)
    late = lax.ppermute(other_late, "blk", swap)
    placed = put_in_order([(own_most, True, most_lists), (early, False, most_lists)], owners, docs, None)
    return put_in_order([(own_late, True, lists), (late, False, lists)], owners, docs, placed)


def passed_along(value, axis, steps):
    count = lax.axis_size(axis)
    pairs = [(source, (source + steps) % count) for source in range(count)]
    return lax.ppermute(value, axis, pairs)


def inverse_factor(gram_sum, counts):
    width_low = gram_sum.shape[1]
    identity_mat = jnp.eye(width_low, dtype=jnp.float32)
    damped = gram_sum / (counts[:, None, None] + 1.0) + identity_mat[None]
    row_bound = jnp.max(jnp.sum(jnp.abs(damped), axis=2), axis=1)
    approx = identity_mat[None] / row_bound[:, None, None]
    for iteration in range(NEWTON_STEPS):
        product = jnp.einsum("dab,dbc->dac", damped, approx, precision=HIGHEST_PRECISION)
        approx = jnp.einsum(
            "dab,dbc->dac", approx, 2.0 * identity_mat[None] - product, precision=HIGHEST_PRECISION
        )
    return approx


def passed(query_inputs, query_grads, proj_in, proj_out, train_rows, token_owner, token_slot):
    tok_count = query_inputs.shape[0]
    width_low = proj_in.shape[1]
    owners = lax.axis_size("blk")
    capacity = 4 * tok_count // owners
    grads_low = jnp.dot(query_grads, proj_out, preferred_element_type=jnp.float32).astype(
        jnp.bfloat16
    )
    inputs_low = jnp.dot(query_inputs, proj_in, preferred_element_type=jnp.float32).astype(
        jnp.bfloat16
    )
    low_rows = jnp.concatenate([grads_low, inputs_low], axis=1)
    owner_ids = token_owner[:, 0]
    owner_hot = (owner_ids[:, None] == jnp.arange(owners, dtype=jnp.int32)[None, :]).astype(
        jnp.float32
    )
    tok_index = jnp.arange(tok_count, dtype=jnp.int32)
    earlier = (tok_index[:, None] > tok_index[None, :]).astype(jnp.float32)
    before = jnp.dot(earlier, owner_hot, precision=HIGHEST_PRECISION)
    rank_in = jnp.sum(before * owner_hot, axis=1).astype(jnp.int32)
    position = owner_ids * capacity + rank_in
    slot_index = jnp.arange(owners * capacity, dtype=jnp.int32)
    placed = slot_index[:, None] == position[None, :]
    send_rows = jnp.dot(
        placed.astype(jnp.bfloat16), low_rows, preferred_element_type=jnp.float32
    ).astype(jnp.bfloat16)
    send_slot = jnp.sum(jnp.where(placed, token_slot[None, :] + 1, 0), axis=1)
    recv_rows, recv_slot = (
        lax.all_to_all(
            send_rows.reshape(owners, capacity, 2 * width_low),
            "blk",
            split_axis=0,
            concat_axis=0,
            tiled=True,
        ),
        lax.all_to_all(
            send_slot.reshape(owners, capacity), "blk", split_axis=0, concat_axis=0, tiled=True
        ),
    )
    recv_rows = recv_rows.reshape(owners * capacity, 2 * width_low)
    recv_slot = recv_slot.reshape(owners * capacity)
    doc_index = jnp.arange(1, DOC_DEV + 1, dtype=jnp.int32)
    doc_hot = recv_slot[:, None] == doc_index[None, :]
    counts = jnp.sum(doc_hot.astype(jnp.float32), axis=0)
    hot_bf = doc_hot.astype(jnp.bfloat16)
    grads_recv = recv_rows[:, :width_low]
    inputs_recv = recv_rows[:, width_low:]
    spread_grads = (hot_bf[:, :, None] * grads_recv[:, None, :]).reshape(
        owners * capacity, DOC_DEV * width_low
    )
    spread_inputs = (hot_bf[:, :, None] * inputs_recv[:, None, :]).reshape(
        owners * capacity, DOC_DEV * width_low
    )
    contract = (((0,), (0,)), ((), ()))
    grad_gram = lax.dot_general(
        spread_grads, recv_rows, contract, preferred_element_type=jnp.float32
    ).reshape(DOC_DEV, width_low, 2 * width_low)
    outer_b = grad_gram[:, :, :width_low]
    doc_grad = grad_gram[:, :, width_low:]
    outer_a = lax.dot_general(
        spread_inputs, inputs_recv, contract, preferred_element_type=jnp.float32
    ).reshape(DOC_DEV, width_low, width_low)
    inv_a = inverse_factor(outer_a, counts)
    inv_b = inverse_factor(outer_b, counts)
    tilted = jnp.einsum("dab,dbc->dac", inv_b, doc_grad, precision=HIGHEST_PRECISION)
    tilted = jnp.einsum("dab,dbc->dac", tilted, inv_a, precision=HIGHEST_PRECISION)
    queries = tilted.reshape(DOC_DEV, width_low * width_low).astype(jnp.bfloat16)
    score_dims = (((1,), (1,)), ((), ()))

    def scoring(block):
        return lax.dot_general(
            block, train_rows, score_dims, preferred_element_type=jnp.float32
        ).astype(jnp.bfloat16)

    def step_ahead(current_block, unused):
        arrived = passed_along(current_block, "blk", 1)
        return (arrived, scoring(arrived))

    def step_back(current_block):
        arrived = passed_along(current_block, "blk", -1)
        return (arrived, scoring(arrived))

    def both_ways(carried, unused):
        ahead_block, back_block = carried
        ahead_block, ahead_tile = step_ahead(ahead_block, unused)
        back_block, back_tile = step_back(back_block)
        return ((ahead_block, back_block), (ahead_tile, back_tile))

    last_pair, paired_tiles = lax.scan(both_ways, (queries, queries), None, length=LEAD)
    ahead_tiles, back_tiles = paired_tiles
    tail_block, tail_tiles = lax.scan(step_ahead, last_pair[0], None, length=STOPS - 1 - 2 * LEAD)
    stacked = jnp.concatenate(
        [jnp.flip(back_tiles, 0), scoring(queries)[None], ahead_tiles, tail_tiles], axis=0
    )
    return stacked


def solution(mesh):
    owners = mesh.shape["blk"]

    def local(query_inputs, query_grads, proj_in, *rest):
        low = proj_in.shape[1]
        cap = 4 * query_inputs.shape[0] // owners
        close = owners % 4 == 0 and STOPS <= owners <= 2 * STOPS and cap == low and cap % TAIL == 0
        return (gathered if close else passed)(query_inputs, query_grads, proj_in, *rest)

    placed = (
        P(("groups", "blk"), None),
        P(("groups", "blk"), None),
        P(),
        P(),
        P(("groups", "blk"), None),
        P(("groups", "blk"), None),
        P(("groups", "blk")),
    )
    return jax.shard_map(
        local,
        mesh=mesh,
        in_specs=placed,
        out_specs=P(None, None, ("groups", "blk")),
        check_vma=False,
    )
```

```python
import functools
import jax
import jax.numpy as jnp
from jax import lax
from jax.experimental import pallas as pl
from jax.experimental.pallas import tpu as pltpu
from jax.sharding import PartitionSpec as P

DOC_DEV = 32
STOPS = 12
NEWTON_STEPS = 6
LEAD = 5
TAIL = 16
GRAM_DOCS = 2
SCORE_COST = 6 * 10**9
F32 = jnp.float32
BF16 = jnp.bfloat16
HIGHEST_PRECISION = lax.Precision.HIGHEST
LAST_DIMS = (((1,), (1,)), ((), ()))


def pack_kernel(
    inputs_hbm, grads_hbm, pin_hbm, pout_hbm, owner_hbm, slot_hbm, send_ref, inputs_ref, grads_ref, pin_ref, pout_ref, owner_ref, slot_ref, sems
):
    owners, per, wide = send_ref.shape
    cap = per - TAIL
    toks, width = inputs_ref.shape
    low = pin_ref.shape[0]
    parts = sems.shape[1] - 1
    part = width // parts
    small = [
        pltpu.make_async_copy(owner_hbm, owner_ref, sems.at[0, parts]),
        pltpu.make_async_copy(slot_hbm, slot_ref, sems.at[1, parts]),
    ]
    large = []
    for i in range(parts):
        at = pl.ds(i * part, part)
        for j, (source, target) in enumerate(
            ((pin_hbm, pin_ref), (inputs_hbm, inputs_ref), (pout_hbm, pout_ref), (grads_hbm, grads_ref))
        ):
            large.append(pltpu.make_async_copy(source.at[:, at], target.at[:, at], sems.at[j, i]))
    for copy in small + large:
        copy.start()

    for copy in small:
        copy.wait()
    owner = owner_ref[...]
    hot = (owner == lax.broadcasted_iota(jnp.int32, (owners, toks), 0)).astype(F32)
    earlier = lax.broadcasted_iota(jnp.int32, (toks, toks), 0) < lax.broadcasted_iota(jnp.int32, (toks, toks), 1)
    before = jnp.dot(hot.astype(BF16), earlier.astype(F32).astype(BF16), preferred_element_type=F32)
    rank = jnp.sum(before * hot, axis=0, keepdims=True).astype(jnp.int32)
    position = owner * cap + rank
    placed = lax.broadcasted_iota(jnp.int32, (owners * cap, toks), 0) == position
    placed = placed.astype(F32).astype(BF16)
    named = (hot * (slot_ref[...].astype(F32) + 1.0)).astype(BF16)
    at_lane = lax.broadcasted_iota(jnp.int32, (wide, toks), 0) % cap == rank
    slots = lax.dot_general(named, at_lane.astype(F32).astype(BF16), LAST_DIMS, preferred_element_type=F32)
    for o in range(owners):
        send_ref[o, cap:, :] = jnp.broadcast_to(slots[o : o + 1], (TAIL, wide)).astype(BF16)

    inputs_low = jnp.zeros((toks, low), F32)
    grads_low = jnp.zeros((toks, low), F32)
    for i in range(parts):
        at = slice(i * part, (i + 1) * part)
        for copy in large[4 * i : 4 * i + 4]:
            copy.wait()
        inputs_low += lax.dot_general(inputs_ref[:, at], pin_ref[:, at], LAST_DIMS, preferred_element_type=F32)
        grads_low += lax.dot_general(grads_ref[:, at], pout_ref[:, at], LAST_DIMS, preferred_element_type=F32)
    both = jnp.concatenate([grads_low, inputs_low], axis=1).astype(BF16)
    rows = jnp.dot(placed, both, preferred_element_type=F32).astype(BF16)
    for o in range(owners):
        send_ref[o, :cap, :] = rows[o * cap : (o + 1) * cap]


def packed_rows(query_inputs, query_grads, proj_in, proj_out, token_owner, token_slot, owners, cap):
    toks, width = query_inputs.shape
    low = proj_in.shape[1]
    return pl.pallas_call(
        pack_kernel,
        out_shape=jax.ShapeDtypeStruct((owners, cap + TAIL, 2 * low), BF16),
        in_specs=[pl.BlockSpec(memory_space=pltpu.HBM)] * 6,
        out_specs=pl.BlockSpec(memory_space=pltpu.VMEM),
        scratch_shapes=[
            pltpu.VMEM((toks, width), BF16),
            pltpu.VMEM((toks, width), BF16),
            pltpu.VMEM((low, width), BF16),
            pltpu.VMEM((low, width), BF16),
            pltpu.VMEM((1, toks), jnp.int32),
            pltpu.VMEM((1, toks), jnp.int32),
            pltpu.SemaphoreType.DMA((4, 5)),
        ],
        compiler_params=pltpu.CompilerParams(vmem_limit_bytes=60 * 2**20),
    )(query_inputs, query_grads, proj_in.T, proj_out.T, token_owner.reshape(1, toks), token_slot.reshape(1, toks))


def split(value, parts):
    out = []
    for _ in range(parts):
        top = value.astype(BF16)
        out.append(top)
        value = value - top.astype(F32)
    return out


def times(left, right):
    rows = left.shape[0]
    parts = split(left, len(right))
    total = None
    for order, piece in enumerate(right):
        used = parts[: len(right) - order]
        got = jnp.dot(jnp.concatenate(used, axis=0), piece, preferred_element_type=F32)
        for j in range(len(used)):
            term = got[j * rows : (j + 1) * rows]
            total = term if total is None else total + term
    return total


def on_diagonal(wide, parts):
    rows = wide.shape[0]
    pair = wide.shape[1] // 2
    first = lax.broadcasted_iota(jnp.int32, (rows, pair), 1) < rows
    zero = jnp.zeros((rows, pair), BF16)
    out = []
    for part in split(wide, parts):
        ahead, after = part[:, :pair], part[:, pair:]
        none = jnp.zeros_like(ahead)
        out.append(
            jnp.concatenate(
                [
                    jnp.concatenate([jnp.where(first, ahead, none), zero], axis=1),
                    jnp.concatenate([jnp.where(first, none, ahead), zero], axis=1),
                    jnp.concatenate([zero, jnp.where(first, after, none)], axis=1),
                    jnp.concatenate([zero, jnp.where(first, none, after)], axis=1),
                ],
                axis=0,
            )
        )
    return out


def query_kernel(first_doc, recv_ref, out_ref, gram_ref, rows_ref, count_ref):
    docs, low, _ = out_ref.shape
    sources, per, wide = recv_ref.shape
    cap = per - TAIL
    rows = jnp.concatenate([recv_ref[s, :cap, :] for s in range(sources)], axis=0)
    rows_ref[...] = rows.T
    half = lax.broadcasted_iota(jnp.int32, (1, wide), 1) < low
    named = [recv_ref[s, cap:, :].astype(F32)[:1] for s in range(sources)]
    slot = jnp.concatenate([jnp.where(half, named[s], named[s + 1]) for s in range(0, sources, 2)], axis=1)
    across = rows_ref[...]
    for d in range(0, docs, GRAM_DOCS):
        picked = []
        for e in range(d, d + GRAM_DOCS):
            mine = (slot == (first_doc + e + 1)).astype(F32)
            picked.append(across * mine.astype(BF16))
            count_ref[e : e + 1, :] = jnp.broadcast_to(jnp.sum(mine, axis=1, keepdims=True), (1, wide))
        gram = jnp.dot(jnp.concatenate(picked, axis=0), rows, preferred_element_type=F32)
        gram_ref[d : d + GRAM_DOCS] = gram.reshape(GRAM_DOCS, wide, wide)

    row_at = lax.broadcasted_iota(jnp.int32, (low, wide), 0)
    lane_at = lax.broadcasted_iota(jnp.int32, (low, wide), 1)
    first = lane_at < low
    eye = ((row_at == lane_at) | (row_at + low == lane_at)).astype(F32)
    eyes = jnp.concatenate([eye, eye], axis=1)
    powers, scales, mixed = [], [], []
    for g in range(0, docs, 2):
        errors, inverses, grads = [], [], []
        for d in (g, g + 1):
            both = gram_ref[d]
            outer = jnp.where(first, both[:low], both[low:])
            damped = outer / (count_ref[d : d + 1, :] + 1.0) + eye
            sums = jnp.sum(jnp.abs(damped), axis=0, keepdims=True)
            bound_b = jnp.max(jnp.where(half, sums, 0.0), axis=1, keepdims=True)
            bound_a = jnp.max(jnp.where(half, 0.0, sums), axis=1, keepdims=True)
            inverse = 1.0 / jnp.where(half, bound_b, bound_a)
            errors.append(eye - damped * inverse)
            inverses.append(inverse)
            grads.append(jnp.where(first, 0.0, both[:low]))
        powers.append(jnp.concatenate(errors, axis=1))
        scales.append(jnp.concatenate(inverses, axis=1))
        mixed.append(grads)
    totals = [eyes + power for power in powers]
    powers = [times(power, on_diagonal(power, 2)) for power in powers]
    for _ in range(NEWTON_STEPS - 2):
        stepped = [
            times(jnp.concatenate([power, total], axis=0), on_diagonal(power, 2))
            for power, total in zip(powers, totals)
        ]
        powers = [both[:low] for both in stepped]
        totals = [total + both[low:] for total, both in zip(totals, stepped)]
    totals = [total + times(total, on_diagonal(power, 2)) for power, total in zip(powers, totals)]
    totals = [total * scale for total, scale in zip(totals, scales)]
    tilted = []
    for total, grads in zip(totals, mixed):
        right = []
        gap = jnp.zeros((low, 2 * wide), BF16)
        zero = jnp.zeros((low, wide), BF16)
        for ahead, after in zip(split(grads[0], 3), split(grads[1], 3)):
            right.append(
                jnp.concatenate(
                    [jnp.concatenate([ahead, zero], axis=1), gap, jnp.concatenate([zero, after], axis=1), gap], axis=0
                )
            )
        tilted.append(times(total, right))
    found = [times(tilt, on_diagonal(total, 3)) for tilt, total in zip(tilted, totals)]
    for g, query in enumerate(found):
        out_ref[2 * g] = query[:, low:wide].astype(BF16)
        out_ref[2 * g + 1] = query[:, wide + low :].astype(BF16)


def queries_of(recv, first_doc, docs, low):
    sources, per, wide = recv.shape
    found = pl.pallas_call(
        functools.partial(query_kernel, first_doc),
        out_shape=jax.ShapeDtypeStruct((docs, low, low), BF16),
        in_specs=[pl.BlockSpec(memory_space=pltpu.VMEM)],
        out_specs=pl.BlockSpec(memory_space=pltpu.VMEM),
        scratch_shapes=[
            pltpu.VMEM((docs, wide, wide), F32),
            pltpu.VMEM((wide, sources * (per - TAIL)), BF16),
            pltpu.VMEM((docs, wide), F32),
        ],
        cost_estimate=pl.CostEstimate(flops=4 * 10**9, bytes_accessed=2**20, transcendentals=0),
        compiler_params=pltpu.CompilerParams(vmem_limit_bytes=16 * 2**20),
    )(recv)
    return found.reshape(docs, low * low)


def score_kernel(count, *refs):
    sets, outs = refs[-2 * count : -count], refs[-count:]
    blocks = jnp.concatenate([ref[...] for ref in refs[: -2 * count]], axis=0)
    for rows, out in zip(sets, outs):
        out[...] = lax.dot_general(blocks, rows[...], LAST_DIMS, preferred_element_type=F32).astype(BF16)


def scores_of(blocks, *sets):
    count = sum(block.shape[0] for block in blocks)
    vmem = pl.BlockSpec(memory_space=pltpu.VMEM)
    return pl.pallas_call(
        functools.partial(score_kernel, len(sets)),
        out_shape=[jax.ShapeDtypeStruct((count, rows.shape[0]), BF16) for rows in sets],
        in_specs=[vmem] * (len(blocks) + len(sets)),
        out_specs=[vmem] * len(sets),
        cost_estimate=pl.CostEstimate(flops=SCORE_COST, bytes_accessed=2**20, transcendentals=0),
        compiler_params=pltpu.CompilerParams(vmem_limit_bytes=16 * 2**20),
    )(*blocks, *sets)


def order_kernel(owners, docs, places, *refs):
    out_ref, sems = refs[-2:]
    chips = owners // 2
    device = lax.axis_index("blk")
    chip, core = lax.div(device, 2), lax.rem(device, 2)
    spot = jnp.where(lax.rem(chip, 2) == 0, lax.div(chip, 2), chips - 1 - lax.div(chip, 2))
    copies = []
    for ref, (own, listed) in zip(refs, places):
        scorer = core if own else 1 - core
        for number, (chunk, hop, partner) in enumerate(listed):
            there = lax.rem(spot + jnp.where(scorer == 0, chips - hop, hop), chips)
            where = jnp.where(there < chips // 2, 2 * there, 2 * (chips - 1 - there) + 1)
            owner = 2 * where + (1 - scorer if partner else scorer)
            stop = lax.rem(device + LEAD - owner + owners, owners)
            wanted = stop < out_ref.shape[0]
            copy = pltpu.make_async_copy(
                ref.at[pl.ds(number * docs, docs), :],
                out_ref.at[jnp.minimum(stop, out_ref.shape[0] - 1), pl.ds(chunk * docs, docs), :],
                sems.at[len(copies)],
            )
            copies.append((wanted, copy))
            pl.when(wanted)(copy.start)
    for wanted, copy in copies:
        pl.when(wanted)(copy.wait)


def put_in_order(tiles, owners, docs, placed):
    refs = [ref for ref, _, _ in tiles]
    places = [(own, listing) for _, own, listing in tiles]
    shape = jax.ShapeDtypeStruct((STOPS, DOC_DEV, refs[0].shape[1]), BF16)
    kernel = functools.partial(order_kernel, owners, docs, places)
    aliases = {}
    if placed is not None:
        aliases = {len(refs): 0}
        refs = refs + [placed]
    specs = [pl.BlockSpec(memory_space=pltpu.VMEM)] * len(tiles) + [pl.BlockSpec(memory_space=pltpu.HBM)] * len(aliases)
    if aliases:
        inner = kernel

        def kernel(*args):
            inner(*args[: len(tiles)], *args[len(tiles) + 1 :])

    return pl.pallas_call(
        kernel,
        out_shape=shape,
        in_specs=specs,
        out_specs=pl.BlockSpec(memory_space=pltpu.HBM),
        input_output_aliases=aliases,
        scratch_shapes=[pltpu.SemaphoreType.DMA((sum(len(listing) for _, _, listing in tiles),))],
        cost_estimate=pl.CostEstimate(flops=1, bytes_accessed=1, transcendentals=0),
        compiler_params=pltpu.CompilerParams(vmem_limit_bytes=4 * 2**20),
    )(*refs)


def ring_pairs(owners):
    chips = owners // 2
    line = chips // 2
    chip_at = [2 * p if p < line else 2 * (chips - 1 - p) + 1 for p in range(chips)]
    pairs = []
    for p in range(chips):
        pairs.append((2 * chip_at[p], 2 * chip_at[(p + 1) % chips]))
        pairs.append((2 * chip_at[p] + 1, 2 * chip_at[(p - 1) % chips] + 1))
    return pairs, [(device, device ^ 1) for device in range(owners)]


def gathered(query_inputs, query_grads, proj_in, proj_out, train_rows, token_owner, token_slot):
    toks = query_inputs.shape[0]
    low = proj_in.shape[1]
    owners = lax.axis_size("blk")
    hops = owners // 4
    train = train_rows.shape[0]
    cap = 4 * toks // owners
    docs = DOC_DEV // 2
    ring, swap = ring_pairs(owners)

    send = packed_rows(query_inputs, query_grads, proj_in, proj_out, token_owner, token_slot, owners, cap)
    recv = lax.all_to_all(send, "blk", split_axis=0, concat_axis=0, tiled=True)

    def ring_on(block, links=ring):
        return lax.ppermute(block, "blk", links)

    following = dict(ring)
    second_next = [(device, following[step]) for device, step in ring]

    first_own = queries_of(recv, 0, docs, low)
    first_next, first_second = ring_on(first_own), ring_on(first_own, second_next)
    first_given = lax.ppermute(first_own, "blk", swap)
    recv, first_own = lax.optimization_barrier((recv, first_own))
    last_own = queries_of(recv, docs, docs, low)
    last_own, first_next, first_second, first_given = lax.optimization_barrier(
        (last_own, first_next, first_second, first_given)
    )
    waiting = [first_own, last_own, first_next, first_second]
    lists = [(0, 0, 0), (1, 0, 0), (0, 1, 0), (0, 2, 0)]
    first = jnp.concatenate([first_second, first_given], axis=0)
    last_given = lax.ppermute(last_own, "blk", swap)
    other_rows = lax.ppermute(lax.optimization_barrier((train_rows, last_given))[0], "blk", swap)
    last = jnp.concatenate([last_own, last_given], axis=0)
    for hop in range(1, hops):
        near = hop < hops - 1
        first = ring_on(first if near else first[docs:])
        arrived = [(0, hop + 2, 0), (0, hop, 1)] if near else [(0, hop, 1)]
        last = ring_on(last)
        if hop == hops - 1:
            most, most_lists, waiting, lists = waiting, lists, [], []
        waiting = waiting + [first, last]
        lists = lists + arrived + [(1, hop, 0), (1, hop, 1)]
    waiting = waiting + [ring_on(last[:docs])]
    lists = lists + [(1, hops, 0)]
    own_most, other_most = scores_of(most, train_rows, other_rows)
    early = lax.ppermute(other_most, "blk", swap)
    placed = put_in_order([(own_most, True, most_lists), (early, False, most_lists)], owners, docs, None)
    waiting[-1], placed = lax.optimization_barrier((waiting[-1], placed))
    (other_late,) = scores_of(waiting, other_rows)
    late = lax.ppermute(other_late, "blk", swap)
    (own_late,) = scores_of(waiting, train_rows)
    return put_in_order([(own_late, True, lists), (late, False, lists)], owners, docs, placed)


def passed_along(value, axis, steps):
    count = lax.axis_size(axis)
    pairs = [(source, (source + steps) % count) for source in range(count)]
    return lax.ppermute(value, axis, pairs)


def inverse_factor(gram_sum, counts):
    width_low = gram_sum.shape[1]
    identity_mat = jnp.eye(width_low, dtype=jnp.float32)
    damped = gram_sum / (counts[:, None, None] + 1.0) + identity_mat[None]
    row_bound = jnp.max(jnp.sum(jnp.abs(damped), axis=2), axis=1)
    approx = identity_mat[None] / row_bound[:, None, None]
    for iteration in range(NEWTON_STEPS):
        product = jnp.einsum("dab,dbc->dac", damped, approx, precision=HIGHEST_PRECISION)
        approx = jnp.einsum(
            "dab,dbc->dac", approx, 2.0 * identity_mat[None] - product, precision=HIGHEST_PRECISION
        )
    return approx


def passed(query_inputs, query_grads, proj_in, proj_out, train_rows, token_owner, token_slot):
    tok_count = query_inputs.shape[0]
    width_low = proj_in.shape[1]
    owners = lax.axis_size("blk")
    capacity = 4 * tok_count // owners
    grads_low = jnp.dot(query_grads, proj_out, preferred_element_type=jnp.float32).astype(
        jnp.bfloat16
    )
    inputs_low = jnp.dot(query_inputs, proj_in, preferred_element_type=jnp.float32).astype(
        jnp.bfloat16
    )
    low_rows = jnp.concatenate([grads_low, inputs_low], axis=1)
    owner_ids = token_owner[:, 0]
    owner_hot = (owner_ids[:, None] == jnp.arange(owners, dtype=jnp.int32)[None, :]).astype(
        jnp.float32
    )
    tok_index = jnp.arange(tok_count, dtype=jnp.int32)
    earlier = (tok_index[:, None] > tok_index[None, :]).astype(jnp.float32)
    before = jnp.dot(earlier, owner_hot, precision=HIGHEST_PRECISION)
    rank_in = jnp.sum(before * owner_hot, axis=1).astype(jnp.int32)
    position = owner_ids * capacity + rank_in
    slot_index = jnp.arange(owners * capacity, dtype=jnp.int32)
    placed = slot_index[:, None] == position[None, :]
    send_rows = jnp.dot(
        placed.astype(jnp.bfloat16), low_rows, preferred_element_type=jnp.float32
    ).astype(jnp.bfloat16)
    send_slot = jnp.sum(jnp.where(placed, token_slot[None, :] + 1, 0), axis=1)
    recv_rows, recv_slot = (
        lax.all_to_all(
            send_rows.reshape(owners, capacity, 2 * width_low),
            "blk",
            split_axis=0,
            concat_axis=0,
            tiled=True,
        ),
        lax.all_to_all(
            send_slot.reshape(owners, capacity), "blk", split_axis=0, concat_axis=0, tiled=True
        ),
    )
    recv_rows = recv_rows.reshape(owners * capacity, 2 * width_low)
    recv_slot = recv_slot.reshape(owners * capacity)
    doc_index = jnp.arange(1, DOC_DEV + 1, dtype=jnp.int32)
    doc_hot = recv_slot[:, None] == doc_index[None, :]
    counts = jnp.sum(doc_hot.astype(jnp.float32), axis=0)
    hot_bf = doc_hot.astype(jnp.bfloat16)
    grads_recv = recv_rows[:, :width_low]
    inputs_recv = recv_rows[:, width_low:]
    spread_grads = (hot_bf[:, :, None] * grads_recv[:, None, :]).reshape(
        owners * capacity, DOC_DEV * width_low
    )
    spread_inputs = (hot_bf[:, :, None] * inputs_recv[:, None, :]).reshape(
        owners * capacity, DOC_DEV * width_low
    )
    contract = (((0,), (0,)), ((), ()))
    grad_gram = lax.dot_general(
        spread_grads, recv_rows, contract, preferred_element_type=jnp.float32
    ).reshape(DOC_DEV, width_low, 2 * width_low)
    outer_b = grad_gram[:, :, :width_low]
    doc_grad = grad_gram[:, :, width_low:]
    outer_a = lax.dot_general(
        spread_inputs, inputs_recv, contract, preferred_element_type=jnp.float32
    ).reshape(DOC_DEV, width_low, width_low)
    inv_a = inverse_factor(outer_a, counts)
    inv_b = inverse_factor(outer_b, counts)
    tilted = jnp.einsum("dab,dbc->dac", inv_b, doc_grad, precision=HIGHEST_PRECISION)
    tilted = jnp.einsum("dab,dbc->dac", tilted, inv_a, precision=HIGHEST_PRECISION)
    queries = tilted.reshape(DOC_DEV, width_low * width_low).astype(jnp.bfloat16)
    score_dims = (((1,), (1,)), ((), ()))

    def scoring(block):
        return lax.dot_general(
            block, train_rows, score_dims, preferred_element_type=jnp.float32
        ).astype(jnp.bfloat16)

    def step_ahead(current_block, unused):
        arrived = passed_along(current_block, "blk", 1)
        return (arrived, scoring(arrived))

    def step_back(current_block):
        arrived = passed_along(current_block, "blk", -1)
        return (arrived, scoring(arrived))

    def both_ways(carried, unused):
        ahead_block, back_block = carried
        ahead_block, ahead_tile = step_ahead(ahead_block, unused)
        back_block, back_tile = step_back(back_block)
        return ((ahead_block, back_block), (ahead_tile, back_tile))

    last_pair, paired_tiles = lax.scan(both_ways, (queries, queries), None, length=LEAD)
    ahead_tiles, back_tiles = paired_tiles
    tail_block, tail_tiles = lax.scan(step_ahead, last_pair[0], None, length=STOPS - 1 - 2 * LEAD)
    stacked = jnp.concatenate(
        [jnp.flip(back_tiles, 0), scoring(queries)[None], ahead_tiles, tail_tiles], axis=0
    )
    return stacked


def solution(mesh):
    owners = mesh.shape["blk"]

    def local(query_inputs, query_grads, proj_in, *rest):
        low = proj_in.shape[1]
        cap = 4 * query_inputs.shape[0] // owners
        close = owners % 4 == 0 and STOPS <= owners <= 2 * STOPS and cap == low and cap % TAIL == 0
        return (gathered if close else passed)(query_inputs, query_grads, proj_in, *rest)

    placed = (
        P(("groups", "blk"), None),
        P(("groups", "blk"), None),
        P(),
        P(),
        P(("groups", "blk"), None),
        P(("groups", "blk"), None),
        P(("groups", "blk")),
    )
    return jax.shard_map(
        local,
        mesh=mesh,
        in_specs=placed,
        out_specs=P(None, None, ("groups", "blk")),
        check_vma=False,
    )
```

```python
import functools
import jax
import jax.numpy as jnp
from jax import lax
from jax.experimental import pallas as pl
from jax.experimental.pallas import tpu as pltpu
from jax.sharding import PartitionSpec as P

DOC_DEV = 32
STOPS = 12
NEWTON_STEPS = 6
LEAD = 5
TAIL = 16
GRAM_DOCS = 2
SCORE_COST = 6 * 10**9
F32 = jnp.float32
BF16 = jnp.bfloat16
HIGHEST_PRECISION = lax.Precision.HIGHEST
LAST_DIMS = (((1,), (1,)), ((), ()))


def pack_kernel(
    inputs_hbm, grads_hbm, pin_hbm, pout_hbm, owner_hbm, slot_hbm, send_ref, inputs_ref, grads_ref, pin_ref, pout_ref, owner_ref, slot_ref, sems
):
    owners, per, wide = send_ref.shape
    cap = per - TAIL
    toks, width = inputs_ref.shape
    low = pin_ref.shape[0]
    parts = sems.shape[1] - 1
    part = width // parts
    small = [
        pltpu.make_async_copy(owner_hbm, owner_ref, sems.at[0, parts]),
        pltpu.make_async_copy(slot_hbm, slot_ref, sems.at[1, parts]),
    ]
    large = []
    for i in range(parts):
        at = pl.ds(i * part, part)
        for j, (source, target) in enumerate(
            ((pin_hbm, pin_ref), (inputs_hbm, inputs_ref), (pout_hbm, pout_ref), (grads_hbm, grads_ref))
        ):
            large.append(pltpu.make_async_copy(source.at[:, at], target.at[:, at], sems.at[j, i]))
    for copy in small + large:
        copy.start()

    for copy in small:
        copy.wait()
    owner = owner_ref[...]
    hot = (owner == lax.broadcasted_iota(jnp.int32, (owners, toks), 0)).astype(F32)
    earlier = lax.broadcasted_iota(jnp.int32, (toks, toks), 0) < lax.broadcasted_iota(jnp.int32, (toks, toks), 1)
    before = jnp.dot(hot.astype(BF16), earlier.astype(F32).astype(BF16), preferred_element_type=F32)
    rank = jnp.sum(before * hot, axis=0, keepdims=True).astype(jnp.int32)
    position = owner * cap + rank
    placed = lax.broadcasted_iota(jnp.int32, (owners * cap, toks), 0) == position
    placed = placed.astype(F32).astype(BF16)
    named = (hot * (slot_ref[...].astype(F32) + 1.0)).astype(BF16)
    at_lane = lax.broadcasted_iota(jnp.int32, (wide, toks), 0) % cap == rank
    slots = lax.dot_general(named, at_lane.astype(F32).astype(BF16), LAST_DIMS, preferred_element_type=F32)
    for o in range(owners):
        send_ref[o, cap:, :] = jnp.broadcast_to(slots[o : o + 1], (TAIL, wide)).astype(BF16)

    inputs_low = jnp.zeros((toks, low), F32)
    grads_low = jnp.zeros((toks, low), F32)
    for i in range(parts):
        at = slice(i * part, (i + 1) * part)
        for copy in large[4 * i : 4 * i + 4]:
            copy.wait()
        inputs_low += lax.dot_general(inputs_ref[:, at], pin_ref[:, at], LAST_DIMS, preferred_element_type=F32)
        grads_low += lax.dot_general(grads_ref[:, at], pout_ref[:, at], LAST_DIMS, preferred_element_type=F32)
    both = jnp.concatenate([grads_low, inputs_low], axis=1).astype(BF16)
    rows = jnp.dot(placed, both, preferred_element_type=F32).astype(BF16)
    for o in range(owners):
        send_ref[o, :cap, :] = rows[o * cap : (o + 1) * cap]


def packed_rows(query_inputs, query_grads, proj_in, proj_out, token_owner, token_slot, owners, cap):
    toks, width = query_inputs.shape
    low = proj_in.shape[1]
    return pl.pallas_call(
        pack_kernel,
        out_shape=jax.ShapeDtypeStruct((owners, cap + TAIL, 2 * low), BF16),
        in_specs=[pl.BlockSpec(memory_space=pltpu.HBM)] * 6,
        out_specs=pl.BlockSpec(memory_space=pltpu.VMEM),
        scratch_shapes=[
            pltpu.VMEM((toks, width), BF16),
            pltpu.VMEM((toks, width), BF16),
            pltpu.VMEM((low, width), BF16),
            pltpu.VMEM((low, width), BF16),
            pltpu.VMEM((1, toks), jnp.int32),
            pltpu.VMEM((1, toks), jnp.int32),
            pltpu.SemaphoreType.DMA((4, 5)),
        ],
        compiler_params=pltpu.CompilerParams(vmem_limit_bytes=60 * 2**20),
    )(query_inputs, query_grads, proj_in.T, proj_out.T, token_owner.reshape(1, toks), token_slot.reshape(1, toks))


def split(value, parts):
    out = []
    for _ in range(parts):
        top = value.astype(BF16)
        out.append(top)
        value = value - top.astype(F32)
    return out


def times(left, right):
    rows = left.shape[0]
    parts = split(left, len(right))
    total = None
    for order, piece in enumerate(right):
        used = parts[: len(right) - order]
        got = jnp.dot(jnp.concatenate(used, axis=0), piece, preferred_element_type=F32)
        for j in range(len(used)):
            term = got[j * rows : (j + 1) * rows]
            total = term if total is None else total + term
    return total


def on_diagonal(wide, parts):
    rows = wide.shape[0]
    pair = wide.shape[1] // 2
    first = lax.broadcasted_iota(jnp.int32, (rows, pair), 1) < rows
    zero = jnp.zeros((rows, pair), BF16)
    out = []
    for part in split(wide, parts):
        ahead, after = part[:, :pair], part[:, pair:]
        none = jnp.zeros_like(ahead)
        out.append(
            jnp.concatenate(
                [
                    jnp.concatenate([jnp.where(first, ahead, none), zero], axis=1),
                    jnp.concatenate([jnp.where(first, none, ahead), zero], axis=1),
                    jnp.concatenate([zero, jnp.where(first, after, none)], axis=1),
                    jnp.concatenate([zero, jnp.where(first, none, after)], axis=1),
                ],
                axis=0,
            )
        )
    return out


def query_kernel(first_doc, recv_ref, out_ref, gram_ref, rows_ref, count_ref):
    docs, low, _ = out_ref.shape
    sources, per, wide = recv_ref.shape
    cap = per - TAIL
    rows = jnp.concatenate([recv_ref[s, :cap, :] for s in range(sources)], axis=0)
    rows_ref[...] = rows.T
    half = lax.broadcasted_iota(jnp.int32, (1, wide), 1) < low
    named = [recv_ref[s, cap:, :].astype(F32)[:1] for s in range(sources)]
    slot = jnp.concatenate([jnp.where(half, named[s], named[s + 1]) for s in range(0, sources, 2)], axis=1)
    across = rows_ref[...]
    for d in range(0, docs, GRAM_DOCS):
        picked = []
        for e in range(d, d + GRAM_DOCS):
            mine = (slot == (first_doc + e + 1)).astype(F32)
            picked.append(across * mine.astype(BF16))
            count_ref[e : e + 1, :] = jnp.broadcast_to(jnp.sum(mine, axis=1, keepdims=True), (1, wide))
        gram = jnp.dot(jnp.concatenate(picked, axis=0), rows, preferred_element_type=F32)
        gram_ref[d : d + GRAM_DOCS] = gram.reshape(GRAM_DOCS, wide, wide)

    row_at = lax.broadcasted_iota(jnp.int32, (low, wide), 0)
    lane_at = lax.broadcasted_iota(jnp.int32, (low, wide), 1)
    first = lane_at < low
    eye = ((row_at == lane_at) | (row_at + low == lane_at)).astype(F32)
    eyes = jnp.concatenate([eye, eye], axis=1)
    powers, scales, mixed = [], [], []
    for g in range(0, docs, 2):
        errors, inverses, grads = [], [], []
        for d in (g, g + 1):
            both = gram_ref[d]
            outer = jnp.where(first, both[:low], both[low:])
            damped = outer / (count_ref[d : d + 1, :] + 1.0) + eye
            sums = jnp.sum(jnp.abs(damped), axis=0, keepdims=True)
            bound_b = jnp.max(jnp.where(half, sums, 0.0), axis=1, keepdims=True)
            bound_a = jnp.max(jnp.where(half, 0.0, sums), axis=1, keepdims=True)
            inverse = 1.0 / jnp.where(half, bound_b, bound_a)
            errors.append(eye - damped * inverse)
            inverses.append(inverse)
            grads.append(jnp.where(first, 0.0, both[:low]))
        powers.append(jnp.concatenate(errors, axis=1))
        scales.append(jnp.concatenate(inverses, axis=1))
        mixed.append(grads)
    totals = [eyes + power for power in powers]
    powers = [times(power, on_diagonal(power, 2)) for power in powers]
    for _ in range(NEWTON_STEPS - 2):
        stepped = [
            times(jnp.concatenate([power, total], axis=0), on_diagonal(power, 2))
            for power, total in zip(powers, totals)
        ]
        powers = [both[:low] for both in stepped]
        totals = [total + both[low:] for total, both in zip(totals, stepped)]
    totals = [total + times(total, on_diagonal(power, 2)) for power, total in zip(powers, totals)]
    totals = [total * scale for total, scale in zip(totals, scales)]
    tilted = []
    for total, grads in zip(totals, mixed):
        right = []
        gap = jnp.zeros((low, 2 * wide), BF16)
        zero = jnp.zeros((low, wide), BF16)
        for ahead, after in zip(split(grads[0], 3), split(grads[1], 3)):
            right.append(
                jnp.concatenate(
                    [jnp.concatenate([ahead, zero], axis=1), gap, jnp.concatenate([zero, after], axis=1), gap], axis=0
                )
            )
        tilted.append(times(total, right))
    found = [times(tilt, on_diagonal(total, 3)) for tilt, total in zip(tilted, totals)]
    for g, query in enumerate(found):
        out_ref[2 * g] = query[:, low:wide].astype(BF16)
        out_ref[2 * g + 1] = query[:, wide + low :].astype(BF16)


def queries_of(recv, first_doc, docs, low):
    sources, per, wide = recv.shape
    found = pl.pallas_call(
        functools.partial(query_kernel, first_doc),
        out_shape=jax.ShapeDtypeStruct((docs, low, low), BF16),
        in_specs=[pl.BlockSpec(memory_space=pltpu.VMEM)],
        out_specs=pl.BlockSpec(memory_space=pltpu.VMEM),
        scratch_shapes=[
            pltpu.VMEM((docs, wide, wide), F32),
            pltpu.VMEM((wide, sources * (per - TAIL)), BF16),
            pltpu.VMEM((docs, wide), F32),
        ],
        cost_estimate=pl.CostEstimate(flops=4 * 10**9, bytes_accessed=2**20, transcendentals=0),
        compiler_params=pltpu.CompilerParams(vmem_limit_bytes=16 * 2**20),
    )(recv)
    return found.reshape(docs, low * low)


def score_kernel(count, *refs):
    sets, outs = refs[-2 * count : -count], refs[-count:]
    blocks = jnp.concatenate([ref[...] for ref in refs[: -2 * count]], axis=0)
    for rows, out in zip(sets, outs):
        out[...] = lax.dot_general(blocks, rows[...], LAST_DIMS, preferred_element_type=F32).astype(BF16)


def scores_of(blocks, *sets):
    count = sum(block.shape[0] for block in blocks)
    vmem = pl.BlockSpec(memory_space=pltpu.VMEM)
    return pl.pallas_call(
        functools.partial(score_kernel, len(sets)),
        out_shape=[jax.ShapeDtypeStruct((count, rows.shape[0]), BF16) for rows in sets],
        in_specs=[vmem] * (len(blocks) + len(sets)),
        out_specs=[vmem] * len(sets),
        cost_estimate=pl.CostEstimate(flops=SCORE_COST, bytes_accessed=2**20, transcendentals=0),
        compiler_params=pltpu.CompilerParams(vmem_limit_bytes=16 * 2**20),
    )(*blocks, *sets)


def order_kernel(owners, docs, places, *refs):
    out_ref, sems = refs[-2:]
    chips = owners // 2
    device = lax.axis_index("blk")
    chip, core = lax.div(device, 2), lax.rem(device, 2)
    spot = jnp.where(lax.rem(chip, 2) == 0, lax.div(chip, 2), chips - 1 - lax.div(chip, 2))
    copies = []
    for ref, (own, listed) in zip(refs, places):
        scorer = core if own else 1 - core
        for number, (chunk, hop, partner) in enumerate(listed):
            there = lax.rem(spot + jnp.where(scorer == 0, chips - hop, hop), chips)
            where = jnp.where(there < chips // 2, 2 * there, 2 * (chips - 1 - there) + 1)
            owner = 2 * where + (1 - scorer if partner else scorer)
            stop = lax.rem(device + LEAD - owner + owners, owners)
            wanted = stop < out_ref.shape[0]
            copy = pltpu.make_async_copy(
                ref.at[pl.ds(number * docs, docs), :],
                out_ref.at[jnp.minimum(stop, out_ref.shape[0] - 1), pl.ds(chunk * docs, docs), :],
                sems.at[len(copies)],
            )
            copies.append((wanted, copy))
            pl.when(wanted)(copy.start)
    for wanted, copy in copies:
        pl.when(wanted)(copy.wait)


def put_in_order(tiles, owners, docs, placed):
    refs = [ref for ref, _, _ in tiles]
    places = [(own, listing) for _, own, listing in tiles]
    shape = jax.ShapeDtypeStruct((STOPS, DOC_DEV, refs[0].shape[1]), BF16)
    kernel = functools.partial(order_kernel, owners, docs, places)
    aliases = {}
    if placed is not None:
        aliases = {len(refs): 0}
        refs = refs + [placed]
    specs = [pl.BlockSpec(memory_space=pltpu.VMEM)] * len(tiles) + [pl.BlockSpec(memory_space=pltpu.HBM)] * len(aliases)
    if aliases:
        inner = kernel

        def kernel(*args):
            inner(*args[: len(tiles)], *args[len(tiles) + 1 :])

    return pl.pallas_call(
        kernel,
        out_shape=shape,
        in_specs=specs,
        out_specs=pl.BlockSpec(memory_space=pltpu.HBM),
        input_output_aliases=aliases,
        scratch_shapes=[pltpu.SemaphoreType.DMA((sum(len(listing) for _, _, listing in tiles),))],
        cost_estimate=pl.CostEstimate(flops=1, bytes_accessed=1, transcendentals=0),
        compiler_params=pltpu.CompilerParams(vmem_limit_bytes=4 * 2**20),
    )(*refs)


def ring_pairs(owners):
    chips = owners // 2
    line = chips // 2
    chip_at = [2 * p if p < line else 2 * (chips - 1 - p) + 1 for p in range(chips)]
    pairs = []
    for p in range(chips):
        pairs.append((2 * chip_at[p], 2 * chip_at[(p + 1) % chips]))
        pairs.append((2 * chip_at[p] + 1, 2 * chip_at[(p - 1) % chips] + 1))
    return pairs, [(device, device ^ 1) for device in range(owners)]


def gathered(query_inputs, query_grads, proj_in, proj_out, train_rows, token_owner, token_slot):
    toks = query_inputs.shape[0]
    low = proj_in.shape[1]
    owners = lax.axis_size("blk")
    hops = owners // 4
    train = train_rows.shape[0]
    cap = 4 * toks // owners
    docs = DOC_DEV // 2
    ring, swap = ring_pairs(owners)

    send = packed_rows(query_inputs, query_grads, proj_in, proj_out, token_owner, token_slot, owners, cap)
    recv = lax.all_to_all(send, "blk", split_axis=0, concat_axis=0, tiled=True)

    def ring_on(block):
        return lax.ppermute(block, "blk", ring)

    first_own = queries_of(recv, 0, docs, low)
    first_next = ring_on(first_own)
    first_given = lax.ppermute(first_own, "blk", swap)
    recv, first_own = lax.optimization_barrier((recv, first_own))
    last_own = queries_of(recv, docs, docs, low)
    last_own, first_next, first_given = lax.optimization_barrier((last_own, first_next, first_given))
    waiting = [first_own, last_own, first_next]
    lists = [(0, 0, 0), (1, 0, 0), (0, 1, 0)]
    first = jnp.concatenate([first_next, first_given], axis=0)
    last_given = lax.ppermute(last_own, "blk", swap)
    other_rows = lax.ppermute(lax.optimization_barrier((train_rows, last_given))[0], "blk", swap)
    last = jnp.concatenate([last_own, last_given], axis=0)
    for hop in range(1, hops):
        near = hop < hops - 1
        first = ring_on(first)
        arrived = [(0, hop + 1, 0), (0, hop, 1)]
        last = ring_on(last)
        if hop == hops - 1:
            most, most_lists, waiting, lists = waiting, lists, [], []
        waiting = waiting + [first, last]
        lists = lists + arrived + [(1, hop, 0), (1, hop, 1)]
    waiting = waiting + [ring_on(last[:docs])]
    lists = lists + [(1, hops, 0)]
    own_most, other_most = scores_of(most, train_rows, other_rows)
    early = lax.ppermute(other_most, "blk", swap)
    placed = put_in_order([(own_most, True, most_lists), (early, False, most_lists)], owners, docs, None)
    waiting[-1], placed = lax.optimization_barrier((waiting[-1], placed))
    (other_late,) = scores_of(waiting, other_rows)
    late = lax.ppermute(other_late, "blk", swap)
    (own_late,) = scores_of(waiting, train_rows)
    return put_in_order([(own_late, True, lists), (late, False, lists)], owners, docs, placed)


def passed_along(value, axis, steps):
    count = lax.axis_size(axis)
    pairs = [(source, (source + steps) % count) for source in range(count)]
    return lax.ppermute(value, axis, pairs)


def inverse_factor(gram_sum, counts):
    width_low = gram_sum.shape[1]
    identity_mat = jnp.eye(width_low, dtype=jnp.float32)
    damped = gram_sum / (counts[:, None, None] + 1.0) + identity_mat[None]
    row_bound = jnp.max(jnp.sum(jnp.abs(damped), axis=2), axis=1)
    approx = identity_mat[None] / row_bound[:, None, None]
    for iteration in range(NEWTON_STEPS):
        product = jnp.einsum("dab,dbc->dac", damped, approx, precision=HIGHEST_PRECISION)
        approx = jnp.einsum(
            "dab,dbc->dac", approx, 2.0 * identity_mat[None] - product, precision=HIGHEST_PRECISION
        )
    return approx


def passed(query_inputs, query_grads, proj_in, proj_out, train_rows, token_owner, token_slot):
    tok_count = query_inputs.shape[0]
    width_low = proj_in.shape[1]
    owners = lax.axis_size("blk")
    capacity = 4 * tok_count // owners
    grads_low = jnp.dot(query_grads, proj_out, preferred_element_type=jnp.float32).astype(
        jnp.bfloat16
    )
    inputs_low = jnp.dot(query_inputs, proj_in, preferred_element_type=jnp.float32).astype(
        jnp.bfloat16
    )
    low_rows = jnp.concatenate([grads_low, inputs_low], axis=1)
    owner_ids = token_owner[:, 0]
    owner_hot = (owner_ids[:, None] == jnp.arange(owners, dtype=jnp.int32)[None, :]).astype(
        jnp.float32
    )
    tok_index = jnp.arange(tok_count, dtype=jnp.int32)
    earlier = (tok_index[:, None] > tok_index[None, :]).astype(jnp.float32)
    before = jnp.dot(earlier, owner_hot, precision=HIGHEST_PRECISION)
    rank_in = jnp.sum(before * owner_hot, axis=1).astype(jnp.int32)
    position = owner_ids * capacity + rank_in
    slot_index = jnp.arange(owners * capacity, dtype=jnp.int32)
    placed = slot_index[:, None] == position[None, :]
    send_rows = jnp.dot(
        placed.astype(jnp.bfloat16), low_rows, preferred_element_type=jnp.float32
    ).astype(jnp.bfloat16)
    send_slot = jnp.sum(jnp.where(placed, token_slot[None, :] + 1, 0), axis=1)
    recv_rows, recv_slot = (
        lax.all_to_all(
            send_rows.reshape(owners, capacity, 2 * width_low),
            "blk",
            split_axis=0,
            concat_axis=0,
            tiled=True,
        ),
        lax.all_to_all(
            send_slot.reshape(owners, capacity), "blk", split_axis=0, concat_axis=0, tiled=True
        ),
    )
    recv_rows = recv_rows.reshape(owners * capacity, 2 * width_low)
    recv_slot = recv_slot.reshape(owners * capacity)
    doc_index = jnp.arange(1, DOC_DEV + 1, dtype=jnp.int32)
    doc_hot = recv_slot[:, None] == doc_index[None, :]
    counts = jnp.sum(doc_hot.astype(jnp.float32), axis=0)
    hot_bf = doc_hot.astype(jnp.bfloat16)
    grads_recv = recv_rows[:, :width_low]
    inputs_recv = recv_rows[:, width_low:]
    spread_grads = (hot_bf[:, :, None] * grads_recv[:, None, :]).reshape(
        owners * capacity, DOC_DEV * width_low
    )
    spread_inputs = (hot_bf[:, :, None] * inputs_recv[:, None, :]).reshape(
        owners * capacity, DOC_DEV * width_low
    )
    contract = (((0,), (0,)), ((), ()))
    grad_gram = lax.dot_general(
        spread_grads, recv_rows, contract, preferred_element_type=jnp.float32
    ).reshape(DOC_DEV, width_low, 2 * width_low)
    outer_b = grad_gram[:, :, :width_low]
    doc_grad = grad_gram[:, :, width_low:]
    outer_a = lax.dot_general(
        spread_inputs, inputs_recv, contract, preferred_element_type=jnp.float32
    ).reshape(DOC_DEV, width_low, width_low)
    inv_a = inverse_factor(outer_a, counts)
    inv_b = inverse_factor(outer_b, counts)
    tilted = jnp.einsum("dab,dbc->dac", inv_b, doc_grad, precision=HIGHEST_PRECISION)
    tilted = jnp.einsum("dab,dbc->dac", tilted, inv_a, precision=HIGHEST_PRECISION)
    queries = tilted.reshape(DOC_DEV, width_low * width_low).astype(jnp.bfloat16)
    score_dims = (((1,), (1,)), ((), ()))

    def scoring(block):
        return lax.dot_general(
            block, train_rows, score_dims, preferred_element_type=jnp.float32
        ).astype(jnp.bfloat16)

    def step_ahead(current_block, unused):
        arrived = passed_along(current_block, "blk", 1)
        return (arrived, scoring(arrived))

    def step_back(current_block):
        arrived = passed_along(current_block, "blk", -1)
        return (arrived, scoring(arrived))

    def both_ways(carried, unused):
        ahead_block, back_block = carried
        ahead_block, ahead_tile = step_ahead(ahead_block, unused)
        back_block, back_tile = step_back(back_block)
        return ((ahead_block, back_block), (ahead_tile, back_tile))

    last_pair, paired_tiles = lax.scan(both_ways, (queries, queries), None, length=LEAD)
    ahead_tiles, back_tiles = paired_tiles
    tail_block, tail_tiles = lax.scan(step_ahead, last_pair[0], None, length=STOPS - 1 - 2 * LEAD)
    stacked = jnp.concatenate(
        [jnp.flip(back_tiles, 0), scoring(queries)[None], ahead_tiles, tail_tiles], axis=0
    )
    return stacked


def solution(mesh):
    owners = mesh.shape["blk"]

    def local(query_inputs, query_grads, proj_in, *rest):
        low = proj_in.shape[1]
        cap = 4 * query_inputs.shape[0] // owners
        close = owners % 4 == 0 and STOPS <= owners <= 2 * STOPS and cap == low and cap % TAIL == 0
        return (gathered if close else passed)(query_inputs, query_grads, proj_in, *rest)

    placed = (
        P(("groups", "blk"), None),
        P(("groups", "blk"), None),
        P(),
        P(),
        P(("groups", "blk"), None),
        P(("groups", "blk"), None),
        P(("groups", "blk")),
    )
    return jax.shard_map(
        local,
        mesh=mesh,
        in_specs=placed,
        out_specs=P(None, None, ("groups", "blk")),
        check_vma=False,
    )
```

```python
import functools
import jax
import jax.numpy as jnp
from jax import lax
from jax.experimental import pallas as pl
from jax.experimental.pallas import tpu as pltpu
from jax.sharding import PartitionSpec as P

DOC_DEV = 32
STOPS = 12
NEWTON_STEPS = 6
LEAD = 5
TAIL = 16
GRAM_DOCS = 2
SCORE_COST = 6 * 10**9
F32 = jnp.float32
BF16 = jnp.bfloat16
HIGHEST_PRECISION = lax.Precision.HIGHEST
LAST_DIMS = (((1,), (1,)), ((), ()))


def pack_kernel(
    inputs_hbm, grads_hbm, pin_hbm, pout_hbm, owner_hbm, slot_hbm, send_ref, inputs_ref, grads_ref, pin_ref, pout_ref, owner_ref, slot_ref, sems
):
    owners, per, wide = send_ref.shape
    cap = per - TAIL
    toks, width = inputs_ref.shape
    low = pin_ref.shape[0]
    parts = sems.shape[1] - 1
    part = width // parts
    small = [
        pltpu.make_async_copy(owner_hbm, owner_ref, sems.at[0, parts]),
        pltpu.make_async_copy(slot_hbm, slot_ref, sems.at[1, parts]),
    ]
    large = []
    for i in range(parts):
        at = pl.ds(i * part, part)
        for j, (source, target) in enumerate(
            ((pin_hbm, pin_ref), (inputs_hbm, inputs_ref), (pout_hbm, pout_ref), (grads_hbm, grads_ref))
        ):
            large.append(pltpu.make_async_copy(source.at[:, at], target.at[:, at], sems.at[j, i]))
    for copy in small + large:
        copy.start()

    for copy in small:
        copy.wait()
    owner = owner_ref[...]
    hot = (owner == lax.broadcasted_iota(jnp.int32, (owners, toks), 0)).astype(F32)
    earlier = lax.broadcasted_iota(jnp.int32, (toks, toks), 0) < lax.broadcasted_iota(jnp.int32, (toks, toks), 1)
    before = jnp.dot(hot.astype(BF16), earlier.astype(F32).astype(BF16), preferred_element_type=F32)
    rank = jnp.sum(before * hot, axis=0, keepdims=True).astype(jnp.int32)
    position = owner * cap + rank
    placed = lax.broadcasted_iota(jnp.int32, (owners * cap, toks), 0) == position
    placed = placed.astype(F32).astype(BF16)
    named = (hot * (slot_ref[...].astype(F32) + 1.0)).astype(BF16)
    at_lane = lax.broadcasted_iota(jnp.int32, (wide, toks), 0) % cap == rank
    slots = lax.dot_general(named, at_lane.astype(F32).astype(BF16), LAST_DIMS, preferred_element_type=F32)
    for o in range(owners):
        send_ref[o, cap:, :] = jnp.broadcast_to(slots[o : o + 1], (TAIL, wide)).astype(BF16)

    inputs_low = jnp.zeros((toks, low), F32)
    grads_low = jnp.zeros((toks, low), F32)
    for i in range(parts):
        at = slice(i * part, (i + 1) * part)
        for copy in large[4 * i : 4 * i + 4]:
            copy.wait()
        inputs_low += lax.dot_general(inputs_ref[:, at], pin_ref[:, at], LAST_DIMS, preferred_element_type=F32)
        grads_low += lax.dot_general(grads_ref[:, at], pout_ref[:, at], LAST_DIMS, preferred_element_type=F32)
    both = jnp.concatenate([grads_low, inputs_low], axis=1).astype(BF16)
    rows = jnp.dot(placed, both, preferred_element_type=F32).astype(BF16)
    for o in range(owners):
        send_ref[o, :cap, :] = rows[o * cap : (o + 1) * cap]


def packed_rows(query_inputs, query_grads, proj_in, proj_out, token_owner, token_slot, owners, cap):
    toks, width = query_inputs.shape
    low = proj_in.shape[1]
    return pl.pallas_call(
        pack_kernel,
        out_shape=jax.ShapeDtypeStruct((owners, cap + TAIL, 2 * low), BF16),
        in_specs=[pl.BlockSpec(memory_space=pltpu.HBM)] * 6,
        out_specs=pl.BlockSpec(memory_space=pltpu.VMEM),
        scratch_shapes=[
            pltpu.VMEM((toks, width), BF16),
            pltpu.VMEM((toks, width), BF16),
            pltpu.VMEM((low, width), BF16),
            pltpu.VMEM((low, width), BF16),
            pltpu.VMEM((1, toks), jnp.int32),
            pltpu.VMEM((1, toks), jnp.int32),
            pltpu.SemaphoreType.DMA((4, 5)),
        ],
        compiler_params=pltpu.CompilerParams(vmem_limit_bytes=60 * 2**20),
    )(query_inputs, query_grads, proj_in.T, proj_out.T, token_owner.reshape(1, toks), token_slot.reshape(1, toks))


def split(value, parts):
    out = []
    for _ in range(parts):
        top = value.astype(BF16)
        out.append(top)
        value = value - top.astype(F32)
    return out


def times(left, right):
    rows = left.shape[0]
    parts = split(left, len(right))
    total = None
    for order, piece in enumerate(right):
        used = parts[: len(right) - order]
        got = jnp.dot(jnp.concatenate(used, axis=0), piece, preferred_element_type=F32)
        for j in range(len(used)):
            term = got[j * rows : (j + 1) * rows]
            total = term if total is None else total + term
    return total


def on_diagonal(wide, parts):
    rows = wide.shape[0]
    pair = wide.shape[1] // 2
    first = lax.broadcasted_iota(jnp.int32, (rows, pair), 1) < rows
    zero = jnp.zeros((rows, pair), BF16)
    out = []
    for part in split(wide, parts):
        ahead, after = part[:, :pair], part[:, pair:]
        none = jnp.zeros_like(ahead)
        out.append(
            jnp.concatenate(
                [
                    jnp.concatenate([jnp.where(first, ahead, none), zero], axis=1),
                    jnp.concatenate([jnp.where(first, none, ahead), zero], axis=1),
                    jnp.concatenate([zero, jnp.where(first, after, none)], axis=1),
                    jnp.concatenate([zero, jnp.where(first, none, after)], axis=1),
                ],
                axis=0,
            )
        )
    return out


def query_kernel(first_doc, recv_ref, out_ref, gram_ref, rows_ref, count_ref):
    docs, low, _ = out_ref.shape
    sources, per, wide = recv_ref.shape
    cap = per - TAIL
    rows = jnp.concatenate([recv_ref[s, :cap, :] for s in range(sources)], axis=0)
    rows_ref[...] = rows.T
    half = lax.broadcasted_iota(jnp.int32, (1, wide), 1) < low
    named = [recv_ref[s, cap:, :].astype(F32)[:1] for s in range(sources)]
    slot = jnp.concatenate([jnp.where(half, named[s], named[s + 1]) for s in range(0, sources, 2)], axis=1)
    across = rows_ref[...]
    for d in range(0, docs, GRAM_DOCS):
        picked = []
        for e in range(d, d + GRAM_DOCS):
            mine = (slot == (first_doc + e + 1)).astype(F32)
            picked.append(across * mine.astype(BF16))
            count_ref[e : e + 1, :] = jnp.broadcast_to(jnp.sum(mine, axis=1, keepdims=True), (1, wide))
        gram = jnp.dot(jnp.concatenate(picked, axis=0), rows, preferred_element_type=F32)
        gram_ref[d : d + GRAM_DOCS] = gram.reshape(GRAM_DOCS, wide, wide)

    row_at = lax.broadcasted_iota(jnp.int32, (low, wide), 0)
    lane_at = lax.broadcasted_iota(jnp.int32, (low, wide), 1)
    first = lane_at < low
    eye = ((row_at == lane_at) | (row_at + low == lane_at)).astype(F32)
    eyes = jnp.concatenate([eye, eye], axis=1)
    powers, scales, mixed = [], [], []
    for g in range(0, docs, 2):
        errors, inverses, grads = [], [], []
        for d in (g, g + 1):
            both = gram_ref[d]
            outer = jnp.where(first, both[:low], both[low:])
            damped = outer / (count_ref[d : d + 1, :] + 1.0) + eye
            sums = jnp.sum(jnp.abs(damped), axis=0, keepdims=True)
            bound_b = jnp.max(jnp.where(half, sums, 0.0), axis=1, keepdims=True)
            bound_a = jnp.max(jnp.where(half, 0.0, sums), axis=1, keepdims=True)
            inverse = 1.0 / jnp.where(half, bound_b, bound_a)
            errors.append(eye - damped * inverse)
            inverses.append(inverse)
            grads.append(jnp.where(first, 0.0, both[:low]))
        powers.append(jnp.concatenate(errors, axis=1))
        scales.append(jnp.concatenate(inverses, axis=1))
        mixed.append(grads)
    totals = [eyes + power for power in powers]
    powers = [times(power, on_diagonal(power, 2)) for power in powers]
    for _ in range(NEWTON_STEPS - 2):
        stepped = [
            times(jnp.concatenate([power, total], axis=0), on_diagonal(power, 2))
            for power, total in zip(powers, totals)
        ]
        powers = [both[:low] for both in stepped]
        totals = [total + both[low:] for total, both in zip(totals, stepped)]
    totals = [total + times(total, on_diagonal(power, 2)) for power, total in zip(powers, totals)]
    totals = [total * scale for total, scale in zip(totals, scales)]
    tilted = []
    for total, grads in zip(totals, mixed):
        right = []
        gap = jnp.zeros((low, 2 * wide), BF16)
        zero = jnp.zeros((low, wide), BF16)
        for ahead, after in zip(split(grads[0], 3), split(grads[1], 3)):
            right.append(
                jnp.concatenate(
                    [jnp.concatenate([ahead, zero], axis=1), gap, jnp.concatenate([zero, after], axis=1), gap], axis=0
                )
            )
        tilted.append(times(total, right))
    found = [times(tilt, on_diagonal(total, 3)) for tilt, total in zip(tilted, totals)]
    for g, query in enumerate(found):
        out_ref[2 * g] = query[:, low:wide].astype(BF16)
        out_ref[2 * g + 1] = query[:, wide + low :].astype(BF16)


def queries_of(recv, first_doc, docs, low):
    sources, per, wide = recv.shape
    found = pl.pallas_call(
        functools.partial(query_kernel, first_doc),
        out_shape=jax.ShapeDtypeStruct((docs, low, low), BF16),
        in_specs=[pl.BlockSpec(memory_space=pltpu.VMEM)],
        out_specs=pl.BlockSpec(memory_space=pltpu.VMEM),
        scratch_shapes=[
            pltpu.VMEM((docs, wide, wide), F32),
            pltpu.VMEM((wide, sources * (per - TAIL)), BF16),
            pltpu.VMEM((docs, wide), F32),
        ],
        cost_estimate=pl.CostEstimate(flops=4 * 10**9, bytes_accessed=2**20, transcendentals=0),
        compiler_params=pltpu.CompilerParams(vmem_limit_bytes=16 * 2**20),
    )(recv)
    return found.reshape(docs, low * low)


def score_kernel(count, *refs):
    sets, outs = refs[-2 * count : -count], refs[-count:]
    blocks = jnp.concatenate([ref[...] for ref in refs[: -2 * count]], axis=0)
    for rows, out in zip(sets, outs):
        out[...] = lax.dot_general(blocks, rows[...], LAST_DIMS, preferred_element_type=F32).astype(BF16)


def scores_of(blocks, *sets):
    count = sum(block.shape[0] for block in blocks)
    vmem = pl.BlockSpec(memory_space=pltpu.VMEM)
    return pl.pallas_call(
        functools.partial(score_kernel, len(sets)),
        out_shape=[jax.ShapeDtypeStruct((count, rows.shape[0]), BF16) for rows in sets],
        in_specs=[vmem] * (len(blocks) + len(sets)),
        out_specs=[vmem] * len(sets),
        cost_estimate=pl.CostEstimate(flops=SCORE_COST, bytes_accessed=2**20, transcendentals=0),
        compiler_params=pltpu.CompilerParams(vmem_limit_bytes=16 * 2**20),
    )(*blocks, *sets)


def order_kernel(owners, docs, places, *refs):
    out_ref, sems = refs[-2:]
    chips = owners // 2
    device = lax.axis_index("blk")
    chip, core = lax.div(device, 2), lax.rem(device, 2)
    spot = jnp.where(lax.rem(chip, 2) == 0, lax.div(chip, 2), chips - 1 - lax.div(chip, 2))
    copies = []
    for ref, (own, listed) in zip(refs, places):
        scorer = core if own else 1 - core
        for number, (chunk, hop, partner) in enumerate(listed):
            there = lax.rem(spot + jnp.where(scorer == 0, chips - hop, hop), chips)
            where = jnp.where(there < chips // 2, 2 * there, 2 * (chips - 1 - there) + 1)
            owner = 2 * where + (1 - scorer if partner else scorer)
            stop = lax.rem(device + LEAD - owner + owners, owners)
            wanted = stop < out_ref.shape[0]
            copy = pltpu.make_async_copy(
                ref.at[pl.ds(number * docs, docs), :],
                out_ref.at[jnp.minimum(stop, out_ref.shape[0] - 1), pl.ds(chunk * docs, docs), :],
                sems.at[len(copies)],
            )
            copies.append((wanted, copy))
            pl.when(wanted)(copy.start)
    for wanted, copy in copies:
        pl.when(wanted)(copy.wait)


def put_in_order(tiles, owners, docs, placed):
    refs = [ref for ref, _, _ in tiles]
    places = [(own, listing) for _, own, listing in tiles]
    shape = jax.ShapeDtypeStruct((STOPS, DOC_DEV, refs[0].shape[1]), BF16)
    kernel = functools.partial(order_kernel, owners, docs, places)
    aliases = {}
    if placed is not None:
        aliases = {len(refs): 0}
        refs = refs + [placed]
    specs = [pl.BlockSpec(memory_space=pltpu.VMEM)] * len(tiles) + [pl.BlockSpec(memory_space=pltpu.HBM)] * len(aliases)
    if aliases:
        inner = kernel

        def kernel(*args):
            inner(*args[: len(tiles)], *args[len(tiles) + 1 :])

    return pl.pallas_call(
        kernel,
        out_shape=shape,
        in_specs=specs,
        out_specs=pl.BlockSpec(memory_space=pltpu.HBM),
        input_output_aliases=aliases,
        scratch_shapes=[pltpu.SemaphoreType.DMA((sum(len(listing) for _, _, listing in tiles),))],
        cost_estimate=pl.CostEstimate(flops=1, bytes_accessed=1, transcendentals=0),
        compiler_params=pltpu.CompilerParams(vmem_limit_bytes=4 * 2**20),
    )(*refs)


def ring_pairs(owners):
    chips = owners // 2
    line = chips // 2
    chip_at = [2 * p if p < line else 2 * (chips - 1 - p) + 1 for p in range(chips)]
    pairs = []
    for p in range(chips):
        pairs.append((2 * chip_at[p], 2 * chip_at[(p + 1) % chips]))
        pairs.append((2 * chip_at[p] + 1, 2 * chip_at[(p - 1) % chips] + 1))
    return pairs, [(device, device ^ 1) for device in range(owners)]


def gathered(query_inputs, query_grads, proj_in, proj_out, train_rows, token_owner, token_slot):
    toks = query_inputs.shape[0]
    low = proj_in.shape[1]
    owners = lax.axis_size("blk")
    hops = owners // 4
    train = train_rows.shape[0]
    cap = 4 * toks // owners
    docs = DOC_DEV // 2
    ring, swap = ring_pairs(owners)

    send = packed_rows(query_inputs, query_grads, proj_in, proj_out, token_owner, token_slot, owners, cap)
    recv = lax.all_to_all(send, "blk", split_axis=0, concat_axis=0, tiled=True)

    def ring_on(block):
        return lax.ppermute(block, "blk", ring)

    first_own = queries_of(recv, 0, docs, low)
    first_next = ring_on(first_own)
    first_given = lax.ppermute(first_own, "blk", swap)
    recv, first_own = lax.optimization_barrier((recv, first_own))
    last_own = queries_of(recv, docs, docs, low)
    last_own, first_next, first_given = lax.optimization_barrier((last_own, first_next, first_given))
    waiting = [first_own, last_own, first_next]
    lists = [(0, 0, 0), (1, 0, 0), (0, 1, 0)]
    first = jnp.concatenate([first_next, first_given], axis=0)
    last_given = lax.ppermute(last_own, "blk", swap)
    other_rows = lax.ppermute(lax.optimization_barrier((train_rows, last_own))[0], "blk", swap)
    last = last_own
    for hop in range(1, hops):
        near = hop < hops - 1
        first = ring_on(first)
        arrived = [(0, hop + 1, 0), (0, hop, 1)]
        last = ring_on(jnp.concatenate([last, last_given], axis=0) if hop == 2 else last)
        if hop == hops - 1:
            most, most_lists, waiting, lists = waiting, lists, [], []
        waiting = waiting + [first, last]
        lists = lists + arrived + [(1, hop, 0)] + ([(1, hop - 1, 1)] if hop > 1 else [])
    waiting = waiting + [ring_on(last)]
    lists = lists + [(1, hops, 0), (1, hops - 1, 1)]
    own_most, other_most = scores_of(most, train_rows, other_rows)
    early = lax.ppermute(other_most, "blk", swap)
    placed = put_in_order([(own_most, True, most_lists), (early, False, most_lists)], owners, docs, None)
    waiting[-1], placed = lax.optimization_barrier((waiting[-1], placed))
    (other_late,) = scores_of(waiting, other_rows)
    late = lax.ppermute(other_late, "blk", swap)
    (own_late,) = scores_of(waiting, train_rows)
    return put_in_order([(own_late, True, lists), (late, False, lists)], owners, docs, placed)


def passed_along(value, axis, steps):
    count = lax.axis_size(axis)
    pairs = [(source, (source + steps) % count) for source in range(count)]
    return lax.ppermute(value, axis, pairs)


def inverse_factor(gram_sum, counts):
    width_low = gram_sum.shape[1]
    identity_mat = jnp.eye(width_low, dtype=jnp.float32)
    damped = gram_sum / (counts[:, None, None] + 1.0) + identity_mat[None]
    row_bound = jnp.max(jnp.sum(jnp.abs(damped), axis=2), axis=1)
    approx = identity_mat[None] / row_bound[:, None, None]
    for iteration in range(NEWTON_STEPS):
        product = jnp.einsum("dab,dbc->dac", damped, approx, precision=HIGHEST_PRECISION)
        approx = jnp.einsum(
            "dab,dbc->dac", approx, 2.0 * identity_mat[None] - product, precision=HIGHEST_PRECISION
        )
    return approx


def passed(query_inputs, query_grads, proj_in, proj_out, train_rows, token_owner, token_slot):
    tok_count = query_inputs.shape[0]
    width_low = proj_in.shape[1]
    owners = lax.axis_size("blk")
    capacity = 4 * tok_count // owners
    grads_low = jnp.dot(query_grads, proj_out, preferred_element_type=jnp.float32).astype(
        jnp.bfloat16
    )
    inputs_low = jnp.dot(query_inputs, proj_in, preferred_element_type=jnp.float32).astype(
        jnp.bfloat16
    )
    low_rows = jnp.concatenate([grads_low, inputs_low], axis=1)
    owner_ids = token_owner[:, 0]
    owner_hot = (owner_ids[:, None] == jnp.arange(owners, dtype=jnp.int32)[None, :]).astype(
        jnp.float32
    )
    tok_index = jnp.arange(tok_count, dtype=jnp.int32)
    earlier = (tok_index[:, None] > tok_index[None, :]).astype(jnp.float32)
    before = jnp.dot(earlier, owner_hot, precision=HIGHEST_PRECISION)
    rank_in = jnp.sum(before * owner_hot, axis=1).astype(jnp.int32)
    position = owner_ids * capacity + rank_in
    slot_index = jnp.arange(owners * capacity, dtype=jnp.int32)
    placed = slot_index[:, None] == position[None, :]
    send_rows = jnp.dot(
        placed.astype(jnp.bfloat16), low_rows, preferred_element_type=jnp.float32
    ).astype(jnp.bfloat16)
    send_slot = jnp.sum(jnp.where(placed, token_slot[None, :] + 1, 0), axis=1)
    recv_rows, recv_slot = (
        lax.all_to_all(
            send_rows.reshape(owners, capacity, 2 * width_low),
            "blk",
            split_axis=0,
            concat_axis=0,
            tiled=True,
        ),
        lax.all_to_all(
            send_slot.reshape(owners, capacity), "blk", split_axis=0, concat_axis=0, tiled=True
        ),
    )
    recv_rows = recv_rows.reshape(owners * capacity, 2 * width_low)
    recv_slot = recv_slot.reshape(owners * capacity)
    doc_index = jnp.arange(1, DOC_DEV + 1, dtype=jnp.int32)
    doc_hot = recv_slot[:, None] == doc_index[None, :]
    counts = jnp.sum(doc_hot.astype(jnp.float32), axis=0)
    hot_bf = doc_hot.astype(jnp.bfloat16)
    grads_recv = recv_rows[:, :width_low]
    inputs_recv = recv_rows[:, width_low:]
    spread_grads = (hot_bf[:, :, None] * grads_recv[:, None, :]).reshape(
        owners * capacity, DOC_DEV * width_low
    )
    spread_inputs = (hot_bf[:, :, None] * inputs_recv[:, None, :]).reshape(
        owners * capacity, DOC_DEV * width_low
    )
    contract = (((0,), (0,)), ((), ()))
    grad_gram = lax.dot_general(
        spread_grads, recv_rows, contract, preferred_element_type=jnp.float32
    ).reshape(DOC_DEV, width_low, 2 * width_low)
    outer_b = grad_gram[:, :, :width_low]
    doc_grad = grad_gram[:, :, width_low:]
    outer_a = lax.dot_general(
        spread_inputs, inputs_recv, contract, preferred_element_type=jnp.float32
    ).reshape(DOC_DEV, width_low, width_low)
    inv_a = inverse_factor(outer_a, counts)
    inv_b = inverse_factor(outer_b, counts)
    tilted = jnp.einsum("dab,dbc->dac", inv_b, doc_grad, precision=HIGHEST_PRECISION)
    tilted = jnp.einsum("dab,dbc->dac", tilted, inv_a, precision=HIGHEST_PRECISION)
    queries = tilted.reshape(DOC_DEV, width_low * width_low).astype(jnp.bfloat16)
    score_dims = (((1,), (1,)), ((), ()))

    def scoring(block):
        return lax.dot_general(
            block, train_rows, score_dims, preferred_element_type=jnp.float32
        ).astype(jnp.bfloat16)

    def step_ahead(current_block, unused):
        arrived = passed_along(current_block, "blk", 1)
        return (arrived, scoring(arrived))

    def step_back(current_block):
        arrived = passed_along(current_block, "blk", -1)
        return (arrived, scoring(arrived))

    def both_ways(carried, unused):
        ahead_block, back_block = carried
        ahead_block, ahead_tile = step_ahead(ahead_block, unused)
        back_block, back_tile = step_back(back_block)
        return ((ahead_block, back_block), (ahead_tile, back_tile))

    last_pair, paired_tiles = lax.scan(both_ways, (queries, queries), None, length=LEAD)
    ahead_tiles, back_tiles = paired_tiles
    tail_block, tail_tiles = lax.scan(step_ahead, last_pair[0], None, length=STOPS - 1 - 2 * LEAD)
    stacked = jnp.concatenate(
        [jnp.flip(back_tiles, 0), scoring(queries)[None], ahead_tiles, tail_tiles], axis=0
    )
    return stacked


def solution(mesh):
    owners = mesh.shape["blk"]

    def local(query_inputs, query_grads, proj_in, *rest):
        low = proj_in.shape[1]
        cap = 4 * query_inputs.shape[0] // owners
        close = owners % 4 == 0 and STOPS <= owners <= 2 * STOPS and cap == low and cap % TAIL == 0
        return (gathered if close else passed)(query_inputs, query_grads, proj_in, *rest)

    placed = (
        P(("groups", "blk"), None),
        P(("groups", "blk"), None),
        P(),
        P(),
        P(("groups", "blk"), None),
        P(("groups", "blk"), None),
        P(("groups", "blk")),
    )
    return jax.shard_map(
        local,
        mesh=mesh,
        in_specs=placed,
        out_specs=P(None, None, ("groups", "blk")),
        check_vma=False,
    )
```

```python
import functools
import jax
import jax.numpy as jnp
from jax import lax
from jax.experimental import pallas as pl
from jax.experimental.pallas import tpu as pltpu
from jax.sharding import PartitionSpec as P

DOC_DEV = 32
STOPS = 12
NEWTON_STEPS = 6
LEAD = 5
TAIL = 16
GRAM_DOCS = 2
SCORE_COST = 6 * 10**9
F32 = jnp.float32
BF16 = jnp.bfloat16
HIGHEST_PRECISION = lax.Precision.HIGHEST
LAST_DIMS = (((1,), (1,)), ((), ()))


def pack_kernel(
    inputs_hbm, grads_hbm, pin_hbm, pout_hbm, owner_hbm, slot_hbm, send_ref, inputs_ref, grads_ref, pin_ref, pout_ref, owner_ref, slot_ref, sems
):
    owners, per, wide = send_ref.shape
    cap = per - TAIL
    toks, width = inputs_ref.shape
    low = pin_ref.shape[0]
    parts = sems.shape[1] - 1
    part = width // parts
    small = [
        pltpu.make_async_copy(owner_hbm, owner_ref, sems.at[0, parts]),
        pltpu.make_async_copy(slot_hbm, slot_ref, sems.at[1, parts]),
    ]
    large = []
    for i in range(parts):
        at = pl.ds(i * part, part)
        for j, (source, target) in enumerate(
            ((pin_hbm, pin_ref), (inputs_hbm, inputs_ref), (pout_hbm, pout_ref), (grads_hbm, grads_ref))
        ):
            large.append(pltpu.make_async_copy(source.at[:, at], target.at[:, at], sems.at[j, i]))
    for copy in small + large:
        copy.start()

    for copy in small:
        copy.wait()
    owner = owner_ref[...]
    hot = (owner == lax.broadcasted_iota(jnp.int32, (owners, toks), 0)).astype(F32)
    earlier = lax.broadcasted_iota(jnp.int32, (toks, toks), 0) < lax.broadcasted_iota(jnp.int32, (toks, toks), 1)
    before = jnp.dot(hot.astype(BF16), earlier.astype(F32).astype(BF16), preferred_element_type=F32)
    rank = jnp.sum(before * hot, axis=0, keepdims=True).astype(jnp.int32)
    position = owner * cap + rank
    placed = lax.broadcasted_iota(jnp.int32, (owners * cap, toks), 0) == position
    placed = placed.astype(F32).astype(BF16)
    named = (hot * (slot_ref[...].astype(F32) + 1.0)).astype(BF16)
    at_lane = lax.broadcasted_iota(jnp.int32, (wide, toks), 0) % cap == rank
    slots = lax.dot_general(named, at_lane.astype(F32).astype(BF16), LAST_DIMS, preferred_element_type=F32)
    for o in range(owners):
        send_ref[o, cap:, :] = jnp.broadcast_to(slots[o : o + 1], (TAIL, wide)).astype(BF16)

    inputs_low = jnp.zeros((toks, low), F32)
    grads_low = jnp.zeros((toks, low), F32)
    for i in range(parts):
        at = slice(i * part, (i + 1) * part)
        for copy in large[4 * i : 4 * i + 4]:
            copy.wait()
        inputs_low += lax.dot_general(inputs_ref[:, at], pin_ref[:, at], LAST_DIMS, preferred_element_type=F32)
        grads_low += lax.dot_general(grads_ref[:, at], pout_ref[:, at], LAST_DIMS, preferred_element_type=F32)
    both = jnp.concatenate([grads_low, inputs_low], axis=1).astype(BF16)
    rows = jnp.dot(placed, both, preferred_element_type=F32).astype(BF16)
    for o in range(owners):
        send_ref[o, :cap, :] = rows[o * cap : (o + 1) * cap]


def packed_rows(query_inputs, query_grads, proj_in, proj_out, token_owner, token_slot, owners, cap):
    toks, width = query_inputs.shape
    low = proj_in.shape[1]
    return pl.pallas_call(
        pack_kernel,
        out_shape=jax.ShapeDtypeStruct((owners, cap + TAIL, 2 * low), BF16),
        in_specs=[pl.BlockSpec(memory_space=pltpu.HBM)] * 6,
        out_specs=pl.BlockSpec(memory_space=pltpu.VMEM),
        scratch_shapes=[
            pltpu.VMEM((toks, width), BF16),
            pltpu.VMEM((toks, width), BF16),
            pltpu.VMEM((low, width), BF16),
            pltpu.VMEM((low, width), BF16),
            pltpu.VMEM((1, toks), jnp.int32),
            pltpu.VMEM((1, toks), jnp.int32),
            pltpu.SemaphoreType.DMA((4, 5)),
        ],
        compiler_params=pltpu.CompilerParams(vmem_limit_bytes=60 * 2**20),
    )(query_inputs, query_grads, proj_in.T, proj_out.T, token_owner.reshape(1, toks), token_slot.reshape(1, toks))


def split(value, parts):
    out = []
    for _ in range(parts):
        top = value.astype(BF16)
        out.append(top)
        value = value - top.astype(F32)
    return out


def times(left, right):
    rows = left.shape[0]
    parts = split(left, len(right))
    total = None
    for order, piece in enumerate(right):
        used = parts[: len(right) - order]
        got = jnp.dot(jnp.concatenate(used, axis=0), piece, preferred_element_type=F32)
        for j in range(len(used)):
            term = got[j * rows : (j + 1) * rows]
            total = term if total is None else total + term
    return total


def on_diagonal(wide, parts):
    rows = wide.shape[0]
    pair = wide.shape[1] // 2
    first = lax.broadcasted_iota(jnp.int32, (rows, pair), 1) < rows
    zero = jnp.zeros((rows, pair), BF16)
    out = []
    for part in split(wide, parts):
        ahead, after = part[:, :pair], part[:, pair:]
        none = jnp.zeros_like(ahead)
        out.append(
            jnp.concatenate(
                [
                    jnp.concatenate([jnp.where(first, ahead, none), zero], axis=1),
                    jnp.concatenate([jnp.where(first, none, ahead), zero], axis=1),
                    jnp.concatenate([zero, jnp.where(first, after, none)], axis=1),
                    jnp.concatenate([zero, jnp.where(first, none, after)], axis=1),
                ],
                axis=0,
            )
        )
    return out


def query_kernel(first_doc, recv_ref, out_ref, gram_ref, rows_ref, count_ref, query_ref):
    docs = out_ref.shape[0]
    sources, per, wide = recv_ref.shape
    low = wide // 2
    cap = per - TAIL
    rows = jnp.concatenate([recv_ref[s, :cap, :] for s in range(sources)], axis=0)
    rows_ref[...] = rows.T
    half = lax.broadcasted_iota(jnp.int32, (1, wide), 1) < low
    named = [recv_ref[s, cap:, :].astype(F32)[:1] for s in range(sources)]
    slot = jnp.concatenate([jnp.where(half, named[s], named[s + 1]) for s in range(0, sources, 2)], axis=1)
    across = rows_ref[...]
    for d in range(0, docs, GRAM_DOCS):
        picked = []
        for e in range(d, d + GRAM_DOCS):
            mine = (slot == (first_doc + e + 1)).astype(F32)
            picked.append(across * mine.astype(BF16))
            count_ref[e : e + 1, :] = jnp.broadcast_to(jnp.sum(mine, axis=1, keepdims=True), (1, wide))
        gram = jnp.dot(jnp.concatenate(picked, axis=0), rows, preferred_element_type=F32)
        gram_ref[d : d + GRAM_DOCS] = gram.reshape(GRAM_DOCS, wide, wide)

    row_at = lax.broadcasted_iota(jnp.int32, (low, wide), 0)
    lane_at = lax.broadcasted_iota(jnp.int32, (low, wide), 1)
    first = lane_at < low
    eye = ((row_at == lane_at) | (row_at + low == lane_at)).astype(F32)
    eyes = jnp.concatenate([eye, eye], axis=1)
    powers, scales, mixed = [], [], []
    for g in range(0, docs, 2):
        errors, inverses, grads = [], [], []
        for d in (g, g + 1):
            both = gram_ref[d]
            outer = jnp.where(first, both[:low], both[low:])
            damped = outer / (count_ref[d : d + 1, :] + 1.0) + eye
            sums = jnp.sum(jnp.abs(damped), axis=0, keepdims=True)
            bound_b = jnp.max(jnp.where(half, sums, 0.0), axis=1, keepdims=True)
            bound_a = jnp.max(jnp.where(half, 0.0, sums), axis=1, keepdims=True)
            inverse = 1.0 / jnp.where(half, bound_b, bound_a)
            errors.append(eye - damped * inverse)
            inverses.append(inverse)
            grads.append(jnp.where(first, 0.0, both[:low]))
        powers.append(jnp.concatenate(errors, axis=1))
        scales.append(jnp.concatenate(inverses, axis=1))
        mixed.append(grads)
    totals = [eyes + power for power in powers]
    powers = [times(power, on_diagonal(power, 2)) for power in powers]
    for _ in range(NEWTON_STEPS - 2):
        stepped = [
            times(jnp.concatenate([power, total], axis=0), on_diagonal(power, 2))
            for power, total in zip(powers, totals)
        ]
        powers = [both[:low] for both in stepped]
        totals = [total + both[low:] for total, both in zip(totals, stepped)]
    totals = [total + times(total, on_diagonal(power, 2)) for power, total in zip(powers, totals)]
    totals = [total * scale for total, scale in zip(totals, scales)]
    tilted = []
    for total, grads in zip(totals, mixed):
        right = []
        gap = jnp.zeros((low, 2 * wide), BF16)
        zero = jnp.zeros((low, wide), BF16)
        for ahead, after in zip(split(grads[0], 3), split(grads[1], 3)):
            right.append(
                jnp.concatenate(
                    [jnp.concatenate([ahead, zero], axis=1), gap, jnp.concatenate([zero, after], axis=1), gap], axis=0
                )
            )
        tilted.append(times(total, right))
    found = [times(tilt, on_diagonal(total, 3)) for tilt, total in zip(tilted, totals)]
    for g, query in enumerate(found):
        query_ref[2 * g * low : (2 * g + 1) * low, :] = query[:, :wide]
        query_ref[(2 * g + 1) * low : (2 * g + 2) * low, :] = query[:, wide:]
    for a in range(0, low, 2):
        even = pltpu.roll(query_ref[pl.ds(a, docs, stride=low), :], low, 1)
        after = query_ref[pl.ds(a + 1, docs, stride=low), :]
        out_ref[:, a * low : (a + 2) * low] = jnp.where(half, even, after).astype(BF16)


def queries_of(recv, first_doc, docs, low):
    sources, per, wide = recv.shape
    return pl.pallas_call(
        functools.partial(query_kernel, first_doc),
        out_shape=jax.ShapeDtypeStruct((docs, low * low), BF16),
        in_specs=[pl.BlockSpec(memory_space=pltpu.VMEM)],
        out_specs=pl.BlockSpec(memory_space=pltpu.VMEM),
        scratch_shapes=[
            pltpu.VMEM((docs, wide, wide), F32),
            pltpu.VMEM((wide, sources * (per - TAIL)), BF16),
            pltpu.VMEM((docs, wide), F32),
            pltpu.VMEM((docs * low, wide), F32),
        ],
        cost_estimate=pl.CostEstimate(flops=4 * 10**9, bytes_accessed=2**20, transcendentals=0),
        compiler_params=pltpu.CompilerParams(vmem_limit_bytes=16 * 2**20),
    )(recv)


def score_kernel(count, *refs):
    sets, outs = refs[-2 * count : -count], refs[-count:]
    blocks = jnp.concatenate([ref[...] for ref in refs[: -2 * count]], axis=0)
    for rows, out in zip(sets, outs):
        out[...] = lax.dot_general(blocks, rows[...], LAST_DIMS, preferred_element_type=F32).astype(BF16)


def scores_of(blocks, *sets):
    count = sum(block.shape[0] for block in blocks)
    vmem = pl.BlockSpec(memory_space=pltpu.VMEM)
    return pl.pallas_call(
        functools.partial(score_kernel, len(sets)),
        out_shape=[jax.ShapeDtypeStruct((count, rows.shape[0]), BF16) for rows in sets],
        in_specs=[vmem] * (len(blocks) + len(sets)),
        out_specs=[vmem] * len(sets),
        cost_estimate=pl.CostEstimate(flops=SCORE_COST, bytes_accessed=2**20, transcendentals=0),
        compiler_params=pltpu.CompilerParams(vmem_limit_bytes=16 * 2**20),
    )(*blocks, *sets)


def order_kernel(owners, docs, places, *refs):
    out_ref, sems = refs[-2:]
    chips = owners // 2
    device = lax.axis_index("blk")
    chip, core = lax.div(device, 2), lax.rem(device, 2)
    spot = jnp.where(lax.rem(chip, 2) == 0, lax.div(chip, 2), chips - 1 - lax.div(chip, 2))
    copies = []
    for ref, (own, listed) in zip(refs, places):
        scorer = core if own else 1 - core
        for number, (chunk, hop, partner) in enumerate(listed):
            there = lax.rem(spot + jnp.where(scorer == 0, chips - hop, hop), chips)
            where = jnp.where(there < chips // 2, 2 * there, 2 * (chips - 1 - there) + 1)
            owner = 2 * where + (1 - scorer if partner else scorer)
            stop = lax.rem(device + LEAD - owner + owners, owners)
            wanted = stop < out_ref.shape[0]
            copy = pltpu.make_async_copy(
                ref.at[pl.ds(number * docs, docs), :],
                out_ref.at[jnp.minimum(stop, out_ref.shape[0] - 1), pl.ds(chunk * docs, docs), :],
                sems.at[len(copies)],
            )
            copies.append((wanted, copy))
            pl.when(wanted)(copy.start)
    for wanted, copy in copies:
        pl.when(wanted)(copy.wait)


def put_in_order(tiles, owners, docs, placed):
    refs = [ref for ref, _, _ in tiles]
    places = [(own, listing) for _, own, listing in tiles]
    shape = jax.ShapeDtypeStruct((STOPS, DOC_DEV, refs[0].shape[1]), BF16)
    kernel = functools.partial(order_kernel, owners, docs, places)
    aliases = {}
    if placed is not None:
        aliases = {len(refs): 0}
        refs = refs + [placed]
    specs = [pl.BlockSpec(memory_space=pltpu.VMEM)] * len(tiles) + [pl.BlockSpec(memory_space=pltpu.HBM)] * len(aliases)
    if aliases:
        inner = kernel

        def kernel(*args):
            inner(*args[: len(tiles)], *args[len(tiles) + 1 :])

    return pl.pallas_call(
        kernel,
        out_shape=shape,
        in_specs=specs,
        out_specs=pl.BlockSpec(memory_space=pltpu.HBM),
        input_output_aliases=aliases,
        scratch_shapes=[pltpu.SemaphoreType.DMA((sum(len(listing) for _, _, listing in tiles),))],
        cost_estimate=pl.CostEstimate(flops=1, bytes_accessed=1, transcendentals=0),
        compiler_params=pltpu.CompilerParams(vmem_limit_bytes=4 * 2**20),
    )(*refs)


def ring_pairs(owners):
    chips = owners // 2
    line = chips // 2
    chip_at = [2 * p if p < line else 2 * (chips - 1 - p) + 1 for p in range(chips)]
    pairs = []
    for p in range(chips):
        pairs.append((2 * chip_at[p], 2 * chip_at[(p + 1) % chips]))
        pairs.append((2 * chip_at[p] + 1, 2 * chip_at[(p - 1) % chips] + 1))
    return pairs, [(device, device ^ 1) for device in range(owners)]


def gathered(query_inputs, query_grads, proj_in, proj_out, train_rows, token_owner, token_slot):
    toks = query_inputs.shape[0]
    low = proj_in.shape[1]
    owners = lax.axis_size("blk")
    hops = owners // 4
    train = train_rows.shape[0]
    cap = 4 * toks // owners
    docs = DOC_DEV // 2
    ring, swap = ring_pairs(owners)

    send = packed_rows(query_inputs, query_grads, proj_in, proj_out, token_owner, token_slot, owners, cap)
    recv = lax.all_to_all(send, "blk", split_axis=0, concat_axis=0, tiled=True)

    def ring_on(block):
        return lax.ppermute(block, "blk", ring)

    first_own = queries_of(recv, 0, docs, low)
    first_next = ring_on(first_own)
    first_given = lax.ppermute(first_own, "blk", swap)
    recv, first_own = lax.optimization_barrier((recv, first_own))
    last_own = queries_of(recv, docs, docs, low)
    last_own, first_next, first_given = lax.optimization_barrier((last_own, first_next, first_given))
    waiting = [first_own, last_own, first_next]
    lists = [(0, 0, 0), (1, 0, 0), (0, 1, 0)]
    first = jnp.concatenate([first_next, first_given], axis=0)
    last_given = lax.ppermute(last_own, "blk", swap)
    other_rows = lax.ppermute(lax.optimization_barrier((train_rows, last_own))[0], "blk", swap)
    last = last_own
    for hop in range(1, hops):
        near = hop < hops - 1
        first = ring_on(first)
        arrived = [(0, hop + 1, 0), (0, hop, 1)]
        last = ring_on(jnp.concatenate([last, last_given], axis=0) if hop == 2 else last)
        if hop == hops - 1:
            most, most_lists, waiting, lists = waiting, lists, [], []
        waiting = waiting + [first, last]
        lists = lists + arrived + [(1, hop, 0)] + ([(1, hop - 1, 1)] if hop > 1 else [])
    waiting = waiting + [ring_on(last)]
    lists = lists + [(1, hops, 0), (1, hops - 1, 1)]
    own_most, other_most = scores_of(most, train_rows, other_rows)
    early = lax.ppermute(other_most, "blk", swap)
    placed = put_in_order([(own_most, True, most_lists), (early, False, most_lists)], owners, docs, None)
    waiting[-1], placed = lax.optimization_barrier((waiting[-1], placed))
    (other_late,) = scores_of(waiting, other_rows)
    late = lax.ppermute(other_late, "blk", swap)
    (own_late,) = scores_of(waiting, train_rows)
    return put_in_order([(own_late, True, lists), (late, False, lists)], owners, docs, placed)


def passed_along(value, axis, steps):
    count = lax.axis_size(axis)
    pairs = [(source, (source + steps) % count) for source in range(count)]
    return lax.ppermute(value, axis, pairs)


def inverse_factor(gram_sum, counts):
    width_low = gram_sum.shape[1]
    identity_mat = jnp.eye(width_low, dtype=jnp.float32)
    damped = gram_sum / (counts[:, None, None] + 1.0) + identity_mat[None]
    row_bound = jnp.max(jnp.sum(jnp.abs(damped), axis=2), axis=1)
    approx = identity_mat[None] / row_bound[:, None, None]
    for iteration in range(NEWTON_STEPS):
        product = jnp.einsum("dab,dbc->dac", damped, approx, precision=HIGHEST_PRECISION)
        approx = jnp.einsum(
            "dab,dbc->dac", approx, 2.0 * identity_mat[None] - product, precision=HIGHEST_PRECISION
        )
    return approx


def passed(query_inputs, query_grads, proj_in, proj_out, train_rows, token_owner, token_slot):
    tok_count = query_inputs.shape[0]
    width_low = proj_in.shape[1]
    owners = lax.axis_size("blk")
    capacity = 4 * tok_count // owners
    grads_low = jnp.dot(query_grads, proj_out, preferred_element_type=jnp.float32).astype(
        jnp.bfloat16
    )
    inputs_low = jnp.dot(query_inputs, proj_in, preferred_element_type=jnp.float32).astype(
        jnp.bfloat16
    )
    low_rows = jnp.concatenate([grads_low, inputs_low], axis=1)
    owner_ids = token_owner[:, 0]
    owner_hot = (owner_ids[:, None] == jnp.arange(owners, dtype=jnp.int32)[None, :]).astype(
        jnp.float32
    )
    tok_index = jnp.arange(tok_count, dtype=jnp.int32)
    earlier = (tok_index[:, None] > tok_index[None, :]).astype(jnp.float32)
    before = jnp.dot(earlier, owner_hot, precision=HIGHEST_PRECISION)
    rank_in = jnp.sum(before * owner_hot, axis=1).astype(jnp.int32)
    position = owner_ids * capacity + rank_in
    slot_index = jnp.arange(owners * capacity, dtype=jnp.int32)
    placed = slot_index[:, None] == position[None, :]
    send_rows = jnp.dot(
        placed.astype(jnp.bfloat16), low_rows, preferred_element_type=jnp.float32
    ).astype(jnp.bfloat16)
    send_slot = jnp.sum(jnp.where(placed, token_slot[None, :] + 1, 0), axis=1)
    recv_rows, recv_slot = (
        lax.all_to_all(
            send_rows.reshape(owners, capacity, 2 * width_low),
            "blk",
            split_axis=0,
            concat_axis=0,
            tiled=True,
        ),
        lax.all_to_all(
            send_slot.reshape(owners, capacity), "blk", split_axis=0, concat_axis=0, tiled=True
        ),
    )
    recv_rows = recv_rows.reshape(owners * capacity, 2 * width_low)
    recv_slot = recv_slot.reshape(owners * capacity)
    doc_index = jnp.arange(1, DOC_DEV + 1, dtype=jnp.int32)
    doc_hot = recv_slot[:, None] == doc_index[None, :]
    counts = jnp.sum(doc_hot.astype(jnp.float32), axis=0)
    hot_bf = doc_hot.astype(jnp.bfloat16)
    grads_recv = recv_rows[:, :width_low]
    inputs_recv = recv_rows[:, width_low:]
    spread_grads = (hot_bf[:, :, None] * grads_recv[:, None, :]).reshape(
        owners * capacity, DOC_DEV * width_low
    )
    spread_inputs = (hot_bf[:, :, None] * inputs_recv[:, None, :]).reshape(
        owners * capacity, DOC_DEV * width_low
    )
    contract = (((0,), (0,)), ((), ()))
    grad_gram = lax.dot_general(
        spread_grads, recv_rows, contract, preferred_element_type=jnp.float32
    ).reshape(DOC_DEV, width_low, 2 * width_low)
    outer_b = grad_gram[:, :, :width_low]
    doc_grad = grad_gram[:, :, width_low:]
    outer_a = lax.dot_general(
        spread_inputs, inputs_recv, contract, preferred_element_type=jnp.float32
    ).reshape(DOC_DEV, width_low, width_low)
    inv_a = inverse_factor(outer_a, counts)
    inv_b = inverse_factor(outer_b, counts)
    tilted = jnp.einsum("dab,dbc->dac", inv_b, doc_grad, precision=HIGHEST_PRECISION)
    tilted = jnp.einsum("dab,dbc->dac", tilted, inv_a, precision=HIGHEST_PRECISION)
    queries = tilted.reshape(DOC_DEV, width_low * width_low).astype(jnp.bfloat16)
    score_dims = (((1,), (1,)), ((), ()))

    def scoring(block):
        return lax.dot_general(
            block, train_rows, score_dims, preferred_element_type=jnp.float32
        ).astype(jnp.bfloat16)

    def step_ahead(current_block, unused):
        arrived = passed_along(current_block, "blk", 1)
        return (arrived, scoring(arrived))

    def step_back(current_block):
        arrived = passed_along(current_block, "blk", -1)
        return (arrived, scoring(arrived))

    def both_ways(carried, unused):
        ahead_block, back_block = carried
        ahead_block, ahead_tile = step_ahead(ahead_block, unused)
        back_block, back_tile = step_back(back_block)
        return ((ahead_block, back_block), (ahead_tile, back_tile))

    last_pair, paired_tiles = lax.scan(both_ways, (queries, queries), None, length=LEAD)
    ahead_tiles, back_tiles = paired_tiles
    tail_block, tail_tiles = lax.scan(step_ahead, last_pair[0], None, length=STOPS - 1 - 2 * LEAD)
    stacked = jnp.concatenate(
        [jnp.flip(back_tiles, 0), scoring(queries)[None], ahead_tiles, tail_tiles], axis=0
    )
    return stacked


def solution(mesh):
    owners = mesh.shape["blk"]

    def local(query_inputs, query_grads, proj_in, *rest):
        low = proj_in.shape[1]
        cap = 4 * query_inputs.shape[0] // owners
        close = owners % 4 == 0 and STOPS <= owners <= 2 * STOPS and cap == low and cap % TAIL == 0
        return (gathered if close else passed)(query_inputs, query_grads, proj_in, *rest)

    placed = (
        P(("groups", "blk"), None),
        P(("groups", "blk"), None),
        P(),
        P(),
        P(("groups", "blk"), None),
        P(("groups", "blk"), None),
        P(("groups", "blk")),
    )
    return jax.shard_map(
        local,
        mesh=mesh,
        in_specs=placed,
        out_specs=P(None, None, ("groups", "blk")),
        check_vma=False,
    )
```
